512 devices in a mesh: row: 16 (over x, y_lo, core), col: 32 (over z, y_hi).
Axes of the slice: x: 4, y: 4 (y_hi: 2, y_lo: 2; y = y_hi * 2 + y_lo), z: 16, core: 2. Of those that a mesh axis runs over, the one named last changes fastest.
Arguments:
- momentum: bfloat16 [3584, 18432], P('row', 'col'), may hold values from -0.020446655 to 0.020446655
Outputs:
- update: bfloat16 [3584, 18432], P('row', 'col')
The draws below stay inside these ranges and needn't reach their ends.
All inputs are finite; a program needn't handle non-finite values.
Results may differ from the reference program's by a relative error of at most 0.0054.
Values may be sent and summed in bfloat16 or wider, within the bound.
A program may use at most 64 MiB of HBM per device.

```python
import jax
import jax.numpy as jnp
from jax import lax

M = 3584
N = 18432


def draw_momentum(key, part):
    key = jax.random.fold_in(key, 7)
    spread = 1.0 / (N ** 0.5 + M ** 0.5)
    values = jnp.clip(jax.random.normal(key, (M, N), jnp.float32), -4.0, 4.0)
    return (values * spread).astype(jnp.bfloat16)


def setup_inputs(seed: int = 0) -> dict:
    streams_of = jax.random.split(jax.random.key(seed), 2)
    momentum = draw_momentum(jax.random.fold_in(streams_of[1], 71), 0)
    return dict(momentum=momentum)


coef_linear = 3.4445
coef_quad = -4.7750
coef_cubic = 2.0315


def reference(momentum):
    whole = momentum.astype(jnp.float32)
    gram = jnp.dot(whole, whole.T, precision=lax.Precision.HIGHEST).astype(jnp.bfloat16)
    gram_wide = gram.astype(jnp.float32)
    square = jnp.dot(gram_wide, gram_wide, precision=lax.Precision.HIGHEST)
    poly = (coef_quad * gram_wide + coef_cubic * square).astype(jnp.bfloat16)
    product = jnp.dot(poly.astype(jnp.float32), whole, precision=lax.Precision.HIGHEST)
    factor = float(max(M, N)) ** 0.5
    return ((coef_linear * whole + product) * factor).astype(jnp.bfloat16)
```

```python
import functools
import math

import jax
import jax.numpy as jnp
from jax import lax
from jax.experimental import pallas as pl
from jax.experimental.pallas import tpu as pltpu
from jax.sharding import PartitionSpec as P

M = 3584
N = 18432

coef_linear = 3.4445
coef_quad = -4.775
coef_cubic = 2.0315

SIDE = 4
DEPTH = 16
BLOCK = M // SIDE
ROWS = BLOCK // SIDE
COLS = N // 32
HALF = BLOCK // 2
CHUNK = 32
USED = HALF // CHUNK
NT = (((1,), (1,)), ((), ()))


def kernel(
    stop, m_ref, out_ref, xi, xj, acc, sib_out, sib_in, plus_out, plus_in, minus_out, minus_in,
    gram, gram_t, t_out, t_in, u, p_out, p_in,
    x_send, x_recv, s_send, s_recv, rs_send, rs_recv, ag_send, ag_recv, f_send, f_recv,
    t_send, t_recv, u_send, u_recv, p_send, p_recv,
):
    row, col = lax.axis_index("row"), lax.axis_index("col")
    x, y_lo, c = row // 4, (row // 2) % 2, row % 2
    z, y_hi = col // 2, col % 2
    y = y_hi * 2 + y_lo
    quarter = y_lo * 2 + c

    def device(x_, y_hi_, y_lo_, z_, c_):
        return ((x_ * 2 + y_lo_) * 2 + c_, z_ * 2 + y_hi_)

    def at(x_, y_, c_):
        return device(x_, y_ // 2, y_ % 2, z, c_)

    def remote(src, dst, send, recv, where):
        return pltpu.make_async_remote_copy(
            src_ref=src, dst_ref=dst, send_sem=send, recv_sem=recv,
            device_id=where, device_id_type=pl.DeviceIdType.MESH,
        )

    def arrived(dst, recv):
        pltpu.make_async_copy(dst, dst, recv).wait()

    sibling = at(x, y, 1 - c)
    right = device(x, y_hi, y_lo, (z + 1) % DEPTH, c)
    left = device(x, y_hi, y_lo, (z + DEPTH - 1) % DEPTH, c)
    own_i = c == y_hi
    own_j = jnp.logical_and(own_i, x == y)

    barrier = pltpu.get_barrier_semaphore()

    def signal(where):
        pl.semaphore_signal(barrier, inc=1, device_id=where, device_id_type=pl.DeviceIdType.MESH)

    def to_i(k):
        return at(x, k, y_hi)

    def from_i(k):
        return at(x, c * 2 + k // 2, k % 2)

    def to_j(k):
        return at(k, x, y_hi)

    def from_j(k):
        return at(y, c * 2 + k // 2, k % 2)

    signal(sibling)
    signal(right)
    signal(left)
    for k in range(SIDE):
        self_i = jnp.logical_and(own_i, y == k)

        @pl.when(jnp.logical_not(self_i))
        def _():
            signal(to_i(k))

        @pl.when(jnp.logical_not(jnp.logical_and(own_i, quarter == k)))
        def _():
            signal(from_i(k))

        @pl.when(jnp.logical_not(jnp.logical_and(own_j, x == k)))
        def _():
            signal(to_j(k))

        @pl.when(jnp.logical_not(jnp.logical_and(own_j, quarter == k)))
        def _():
            signal(from_j(k))

        if k:
            signal(at((x + k) % SIDE, y, c))
    count = 3 + 4 * SIDE + SIDE - 1
    pl.semaphore_wait(
        barrier, count - 2 * own_i.astype(jnp.int32) - 2 * own_j.astype(jnp.int32)
    )

    def x_copies(k):
        to_a = (y + 1 + k) % SIDE
        to_b = (x + 1 + k) % SIDE
        a = (m_ref, xi.at[quarter], x_send.at[0, k], x_recv.at[0, quarter])
        b = (m_ref, xj.at[quarter], x_send.at[1, k], x_recv.at[1, quarter])
        return (
            (a, to_i(to_a), jnp.logical_and(own_i, k == SIDE - 1)),
            (b, to_j(to_b), jnp.logical_and(own_j, k == SIDE - 1)),
        )

    for k in range(SIDE):
        for (src, dst, send, recv), where, local in x_copies(k):

            @pl.when(local)
            def _():
                pltpu.make_async_copy(src, dst, recv).start()

            @pl.when(jnp.logical_not(local))
            def _():
                remote(src, dst, send, recv, where).start()

    acc[USED:] = jnp.zeros_like(acc[USED:])
    for k in range(SIDE):
        arrived(xi.at[k], x_recv.at[0, k])
        arrived(xj.at[k], x_recv.at[1, k])

    def finish_x():
        for k in range(SIDE):
            for (src, dst, send, recv), where, local in x_copies(k):

                @pl.when(jnp.logical_not(local))
                def _():
                    remote(src, dst, send, recv, where).wait_send()

    if stop == 1:
        finish_x()
        out_ref[...] = xi[0] + xj[0]
        return

    xi_all = xi[...].reshape(BLOCK, COLS)
    for k in range(2):
        part = lax.dot_general(
            xj[(1 - c) * 2 + k], xi_all, NT, preferred_element_type=jnp.float32
        )
        sib_out[k] = part.astype(jnp.bfloat16)
        remote(sib_out.at[k], sib_in.at[k], s_send.at[k], s_recv.at[k], sibling).start()
    for k in range(2):
        part = lax.dot_general(xj[c * 2 + k], xi_all, NT, preferred_element_type=jnp.float32)
        acc[k * 7 : (k + 1) * 7] = part.reshape(7, CHUNK, BLOCK)
    for k in range(2):
        remote(sib_out.at[k], sib_in.at[k], s_send.at[k], s_recv.at[k], sibling).wait()
        acc[k * 7 : (k + 1) * 7] += sib_in[k].reshape(7, CHUNK, BLOCK).astype(jnp.float32)

    if stop == 2:
        finish_x()
        out_ref[...] = acc[0:7].reshape(ROWS, BLOCK)[:, :COLS].astype(jnp.bfloat16)
        return

    def plus(s):
        return remote(plus_out.at[s], plus_in.at[s], rs_send.at[0, s], rs_recv.at[0, s], right)

    def minus(s):
        return remote(minus_out.at[s], minus_in.at[s], rs_send.at[1, s], rs_recv.at[1, s], left)

    plus_out[0] = acc[(z + 8) % DEPTH].astype(jnp.bfloat16)
    plus(0).start()
    minus_out[0] = acc[(z + DEPTH - 7) % DEPTH].astype(jnp.bfloat16)
    minus(0).start()

    def rs_plus(s):
        plus(s - 1).wait_recv()
        o = (z + 8 - s) % DEPTH
        plus_out[s] = (acc[o] + plus_in[s - 1].astype(jnp.float32)).astype(jnp.bfloat16)
        plus(s).start()

    def rs_minus(s):
        minus(s - 1).wait_recv()
        o = (z + DEPTH - 7 + s) % DEPTH
        minus_out[s] = (acc[o] + minus_in[s - 1].astype(jnp.float32)).astype(jnp.bfloat16)
        minus(s).start()

    @pl.loop(1, 7)
    def _(s):
        rs_plus(s)
        rs_minus(s)

    rs_plus(7)
    minus(6).wait_recv()
    plus(7).wait_recv()

    def slot(core, o):
        return jnp.where(o < USED, core * USED + o, 2 * USED + core * 2 + o - USED)

    total = acc[z] + plus_in[7].astype(jnp.float32) + minus_in[6].astype(jnp.float32)
    gram[slot(c, z)] = total.astype(jnp.bfloat16)

    def finish_rs():
        @pl.loop(0, 7)
        def _(s):
            plus(s).wait_send()
            minus(s).wait_send()

        plus(7).wait_send()

    if stop == 3:
        finish_x()
        finish_rs()
        out_ref[0:32] = gram[slot(c, z)][:, :COLS]
        return

    def ag_plus(s):
        k = slot(c, (z + DEPTH - s) % DEPTH)
        return remote(gram.at[k], gram.at[k], ag_send.at[0, s], ag_recv.at[0, s], right)

    def ag_minus(s):
        k = slot(c, (z + s) % DEPTH)
        return remote(gram.at[k], gram.at[k], ag_send.at[1, s], ag_recv.at[1, s], left)

    def ag_plus_in(s):
        arrived(gram.at[slot(c, (z + DEPTH - 1 - s) % DEPTH)], ag_recv.at[0, s])

    def ag_minus_in(s):
        arrived(gram.at[slot(c, (z + 1 + s) % DEPTH)], ag_recv.at[1, s])

    def hand(o):
        k = slot(c, o)
        return remote(gram.at[k], gram.at[k], f_send.at[o], f_recv.at[o], sibling)

    ag_plus(0).start()
    ag_minus(0).start()
    hand(z).start()

    @pl.loop(1, 7)
    def _(s):
        ag_plus_in(s - 1)
        ag_plus(s).start()
        hand((z + DEPTH - s) % DEPTH).start()
        ag_minus_in(s - 1)
        ag_minus(s).start()
        hand((z + s) % DEPTH).start()

    ag_plus_in(6)
    ag_plus(7).start()
    hand((z + DEPTH - 7) % DEPTH).start()
    ag_minus_in(6)
    hand((z + 7) % DEPTH).start()
    ag_plus_in(7)
    hand((z + 8) % DEPTH).start()

    @pl.loop(0, DEPTH)
    def _(o):
        arrived(gram.at[slot(1 - c, o)], f_recv.at[o])

    def finish_ag():
        @pl.loop(0, 7)
        def _(s):
            ag_plus(s).wait_send()
            ag_minus(s).wait_send()

        ag_plus(7).wait_send()

        @pl.loop(0, DEPTH)
        def _(o):
            hand(o).wait_send()

    if stop == 4:
        finish_x()
        finish_rs()
        finish_ag()
        out_ref[...] = gram[0:7].reshape(ROWS, BLOCK)[:, :COLS]
        return

    def t_part(q):
        return jnp.dot(
            gram[pl.ds(q * 7, 7)].reshape(ROWS, BLOCK), xi_all, preferred_element_type=jnp.float32
        )

    def t_copy(k):
        where = at((x + k) % SIDE, y, c)
        return remote(t_out.at[k], t_in.at[k], t_send.at[k], t_recv.at[k], where)

    for k in (2, 1, 3):
        t_out[k] = t_part((x + k) % SIDE).astype(jnp.bfloat16)
        t_copy(k).start()
    t_sum = t_part(x)
    gram_t[...] = gram[0 : 2 * USED].reshape(BLOCK, BLOCK).T.reshape(SIDE, ROWS, BLOCK)
    for k in (1, 3, 2):
        t_copy(k).wait_recv()
        t_sum += t_in[k].astype(jnp.float32)

    u[x] = (coef_quad * xj[x].astype(jnp.float32) + coef_cubic * t_sum).astype(jnp.bfloat16)

    def u_copy(k):
        where = at((x + k) % SIDE, y, c)
        return remote(u.at[x], u.at[x], u_send.at[k], u_recv.at[k], where)

    for k in (2, 1, 3):
        u_copy(k).start()
    for k in (1, 3, 2):
        arrived(u.at[(x + SIDE - k) % SIDE], u_recv.at[k])

    def finish_u():
        for k in (1, 2, 3):
            t_copy(k).wait_send()
            u_copy(k).wait_send()

    if stop == 5:
        finish_x()
        finish_rs()
        finish_ag()
        finish_u()
        out_ref[...] = u[0] + u[1] + u[2] + u[3] + gram_t[0, :, :COLS]
        return

    u_all = u[...].reshape(BLOCK, COLS)

    def p_copy(q):
        return remote(p_out.at[q], p_in.at[y], p_send.at[q], p_recv.at[y], from_i(q))

    for q in range(SIDE):
        local = jnp.logical_and(own_i, q == quarter)
        p_out[q] = jnp.dot(gram_t[q], u_all, preferred_element_type=jnp.float32).astype(
            jnp.bfloat16
        )

        @pl.when(local)
        def _():
            pltpu.make_async_copy(p_out.at[q], p_in.at[y], p_recv.at[y]).start()

        @pl.when(jnp.logical_not(local))
        def _():
            p_copy(q).start()

    finish_x()
    finish_rs()
    finish_ag()
    finish_u()
    result = coef_linear * m_ref[...].astype(jnp.float32)
    for k in range(SIDE):
        arrived(p_in.at[k], p_recv.at[k])
        result += p_in[k].astype(jnp.float32)
    out_ref[...] = (result * math.sqrt(max(M, N))).astype(jnp.bfloat16)
    for q in range(SIDE):

        @pl.when(jnp.logical_not(jnp.logical_and(own_i, q == quarter)))
        def _():
            p_copy(q).wait_send()


def body(momentum, stop=0):
    bf16, f32 = jnp.bfloat16, jnp.float32
    block = (SIDE, ROWS, COLS)
    ring = (8, CHUNK, BLOCK)
    sem = pltpu.SemaphoreType.DMA
    return pl.pallas_call(
        functools.partial(kernel, stop),
        out_shape=jax.ShapeDtypeStruct((ROWS, COLS), bf16),
        in_specs=[pl.BlockSpec(memory_space=pltpu.VMEM)],
        out_specs=pl.BlockSpec(memory_space=pltpu.VMEM),
        scratch_shapes=[
            pltpu.VMEM(block, bf16),
            pltpu.VMEM(block, bf16),
            pltpu.VMEM((DEPTH, CHUNK, BLOCK), f32),
            pltpu.VMEM((2, ROWS, BLOCK), bf16),
            pltpu.VMEM((2, ROWS, BLOCK), bf16),
            pltpu.VMEM(ring, bf16),
            pltpu.VMEM(ring, bf16),
            pltpu.VMEM(ring, bf16),
            pltpu.VMEM(ring, bf16),
            pltpu.VMEM((2 * DEPTH, CHUNK, BLOCK), bf16),
            pltpu.VMEM((SIDE, ROWS, BLOCK), bf16),
            pltpu.VMEM(block, bf16),
            pltpu.VMEM(block, bf16),
            pltpu.VMEM(block, bf16),
            pltpu.VMEM(block, bf16),
            pltpu.VMEM(block, bf16),
            sem((2, SIDE)), sem((2, SIDE)),
            sem((2,)), sem((2,)),
            sem((2, 8)), sem((2, 8)),
            sem((2, 8)), sem((2, 8)),
            sem((DEPTH,)), sem((DEPTH,)),
            sem((SIDE,)), sem((SIDE,)),
            sem((SIDE,)), sem((SIDE,)),
            sem((SIDE,)), sem((SIDE,)),
        ],
        compiler_params=pltpu.CompilerParams(
            collective_id=0, has_side_effects=True, vmem_limit_bytes=48 * 2**20
        ),
        cost_estimate=pl.CostEstimate(
            flops=6 * BLOCK * BLOCK * COLS, bytes_accessed=4 * ROWS * COLS, transcendentals=0
        ),
        name="newton_schulz",
    )(momentum)


def solution(mesh):
    return jax.shard_map(
        body,
        mesh=mesh,
        in_specs=(P("row", "col"),),
        out_specs=P("row", "col"),
        check_vma=False,
    )
```

```python
import functools
import math

import jax
import jax.numpy as jnp
from jax import lax
from jax.experimental import pallas as pl
from jax.experimental.pallas import tpu as pltpu
from jax.sharding import PartitionSpec as P

M = 3584
N = 18432

coef_linear = 3.4445
coef_quad = -4.775
coef_cubic = 2.0315

SIDE = 4
DEPTH = 16
BLOCK = M // SIDE
ROWS = BLOCK // SIDE
COLS = N // 32
PART = ROWS // 2
PIECE = 32
PADDED = 4 * PIECE
GROUPS = ((0, 256), (256, COLS - 256))
NT = (((1,), (1,)), ((), ()))


def kernel(
    stop, m_ref, out_ref, xi, xj, acc, sib_out, sib_in, near_out, near_in, cls, far_out, far_in,
    gram, gram_t, t_out, t_in, t_sum, u, p_out, p_in,
    i_send, i_recv, j_send, j_recv, s_send, s_recv, near_send, near_recv, far_send, far_recv,
    gf_send, gf_recv, gn_send, gn_recv, h_send, h_recv,
    t_send, t_recv, u_send, u_recv, p_send, p_recv,
):
    row, col = lax.axis_index("row"), lax.axis_index("col")
    x, y_lo, c = row // 4, (row // 2) % 2, row % 2
    z, y_hi = col // 2, col % 2
    y = y_hi * 2 + y_lo
    quarter = y_lo * 2 + c
    r, a = z % 4, z // 4
    bf16, f32 = jnp.bfloat16, jnp.float32

    def at(x_, y_, c_):
        return ((x_ * 2 + y_ % 2) * 2 + c_, z * 2 + y_ // 2)

    def along(d):
        return (row, ((z + d + DEPTH) % DEPTH) * 2 + y_hi)

    def remote(src, dst, send, recv, where):
        return pltpu.make_async_remote_copy(
            src_ref=src, dst_ref=dst, send_sem=send, recv_sem=recv,
            device_id=where, device_id_type=pl.DeviceIdType.MESH,
        )

    def arrived(dst, recv):
        pltpu.make_async_copy(dst, dst, recv).wait()

    def to_i(k):
        return at(x, k, y_hi)

    def from_i(k):
        return at(x, c * 2 + k // 2, k % 2)

    sibling = at(x, y, 1 - c)
    partner = at(x, c * 2 + y_lo, y_hi)
    own = c == y_hi
    others = jnp.logical_not(own)
    near = (1, -1, 2 - 4 * c)

    barrier = pltpu.get_barrier_semaphore()

    def signal(where):
        pl.semaphore_signal(barrier, inc=1, device_id=where, device_id_type=pl.DeviceIdType.MESH)

    signal(sibling)
    for d in (1, -1, 2, -2, 4, -4, 8):
        signal(along(d))
    for k in (1, 2, 3):
        signal(at((x + k) % SIDE, y, c))
    for k in range(SIDE):

        @pl.when(jnp.logical_not(jnp.logical_and(own, y == k)))
        def _():
            signal(to_i(k))

        @pl.when(jnp.logical_not(jnp.logical_and(own, quarter == k)))
        def _():
            signal(from_i(k))

    @pl.when(others)
    def _():
        signal(partner)

    pl.semaphore_wait(barrier, 20 - 3 * own.astype(jnp.int32))

    def j_first():
        return remote(m_ref, xj.at[x], j_send.at[0], j_recv.at[0], partner)

    def i_copy(k):
        return remote(
            m_ref, xi.at[quarter], i_send.at[k], i_recv.at[quarter], to_i((y + k) % SIDE)
        )

    def j_copy(k):
        where = at((x + k) % SIDE, y, c)
        return remote(xj.at[x], xj.at[x], j_send.at[k], j_recv.at[k], where)

    @pl.when(own)
    def _():
        pltpu.make_async_copy(m_ref, xj.at[x], j_recv.at[0]).start()
        pltpu.make_async_copy(m_ref, xi.at[quarter], i_recv.at[quarter]).start()

    @pl.when(others)
    def _():
        j_first().start()
        i_copy(0).start()

    for k in (2, 1, 3):
        i_copy(k).start()
    arrived(xj.at[x], j_recv.at[0])
    for k in (2, 1, 3):
        j_copy(k).start()
    for k in range(SIDE):
        arrived(xi.at[k], i_recv.at[k])
    for k in (1, 2, 3):
        arrived(xj.at[(x + SIDE - k) % SIDE], j_recv.at[k])

    def finish():
        @pl.when(others)
        def _():
            j_first().wait_send()
            i_copy(0).wait_send()

        for k in (1, 2, 3):
            i_copy(k).wait_send()
            j_copy(k).wait_send()
        if stop == 1:
            return
        for k in range(2):
            s_copy(k).wait_send()
        if stop == 2:
            return
        for k in range(3):
            near_copy(k).wait_send()
            far_copy(k).wait_send()
        if stop == 3:
            return
        for k in range(3):
            gf_copy(k).wait_send()
            gn_copy(k).wait_send()
        for k in range(4):
            hand(k).wait_send()
        if stop == 4:
            return
        for g in range(2):
            for k in (1, 2, 3):
                t_copy(g, k).wait_send()
                u_copy(g, k).wait_send()

    if stop == 1:
        finish()
        out_ref[...] = xi[0] + xj[0]
        return

    def s_copy(k):
        part = pl.ds(2 * k, 2)
        return remote(sib_out.at[part], sib_in.at[part], s_send.at[k], s_recv.at[k], sibling)

    xi_all = xi[...].reshape(BLOCK, COLS)
    for k in range(2):
        term = lax.dot_general(xj[(1 - c) * 2 + k], xi_all, NT, preferred_element_type=f32)
        sib_out[2 * k : 2 * k + 2] = term.astype(bf16).reshape(2, PART, BLOCK)
        s_copy(k).start()
    for k in range(2):
        term = lax.dot_general(xj[c * 2 + k], xi_all, NT, preferred_element_type=f32)
        acc[2 * k : 2 * k + 2] = term.reshape(2, PART, BLOCK)
    for k in range(2):
        s_copy(k).wait_recv()

    if stop == 2:
        finish()
        out_ref[0:PART] = (acc[0] + sib_in[0].astype(f32))[:, :COLS].astype(bf16)
        return

    def near_copy(k):
        return remote(
            near_out.at[k], near_in.at[k], near_send.at[k], near_recv.at[k], along(near[k])
        )

    for k in (2, 0, 1):
        q = (r + near[k] + 4) % 4
        near_out[k] = (acc[q] + sib_in[q].astype(f32)).astype(bf16)
        near_copy(k).start()
    cls[0:PART] = acc[r] + sib_in[r].astype(f32)
    cls[PART:] = jnp.zeros_like(cls[PART:])
    for k in (0, 1, 2):
        near_copy(k).wait_recv()
        cls[0:PART] += near_in[k].astype(f32)
    far_out[...] = cls[...].astype(bf16)

    def far_copy(k):
        piece = pl.ds(((a + k + 1) % 4) * PIECE, PIECE)
        where = along(4 * (k + 1))
        return remote(far_out.at[piece], far_in.at[k], far_send.at[k], far_recv.at[k], where)

    for k in (1, 0, 2):
        far_copy(k).start()
    total = cls[pl.ds(a * PIECE, PIECE)]
    for k in (0, 2, 1):
        far_copy(k).wait_recv()
        total += far_in[k].astype(f32)
    gram[c, r, pl.ds(a * PIECE, PIECE)] = total.astype(bf16)

    if stop == 3:
        finish()
        out_ref[0:PIECE] = gram[c, r, pl.ds(a * PIECE, PIECE)][:, :COLS]
        return

    def gf_copy(k):
        piece = gram.at[c, r, pl.ds(a * PIECE, PIECE)]
        return remote(piece, piece, gf_send.at[k], gf_recv.at[k], along(4 * (k + 1)))

    def gn_copy(k):
        part = gram.at[c, r, pl.ds(0, PART)]
        return remote(part, part, gn_send.at[k], gn_recv.at[k], along(near[k]))

    def hand(k):
        part = gram.at[c, (r + k) % 4, pl.ds(0, PART)]
        return remote(part, part, h_send.at[k], h_recv.at[k], sibling)

    for k in (1, 0, 2):
        gf_copy(k).start()
    for k in (0, 2, 1):
        arrived(gram.at[c, r, pl.ds(((a + 3 - k) % 4) * PIECE, PIECE)], gf_recv.at[k])
    for k in (2, 0, 1):
        gn_copy(k).start()
    hand(0).start()
    for k in (0, 1, 2):
        arrived(gram.at[c, (r - near[k] + 4) % 4, pl.ds(0, PART)], gn_recv.at[k])
        hand((3, 1, 2)[k]).start()
    for k in range(4):
        arrived(gram.at[1 - c, (r + k) % 4, pl.ds(0, PART)], h_recv.at[k])

    if stop == 4:
        finish()
        out_ref[0:PART] = gram[0, 0, 0:PART, :COLS]
        return

    def columns(g):
        return pl.ds(*GROUPS[g])

    def t_part(g, q):
        rows = gram[q // 2, pl.ds((q % 2) * 2, 2), 0:PART].reshape(ROWS, BLOCK)
        right = xi[:, :, columns(g)].reshape(BLOCK, GROUPS[g][1])
        return jnp.dot(rows, right, preferred_element_type=f32)

    def t_copy(g, k):
        where = at((x + k) % SIDE, y, c)
        part = columns(g)
        return remote(
            t_out.at[k, :, part], t_in.at[k, :, part], t_send.at[g, k], t_recv.at[g, k], where
        )

    def u_copy(g, k):
        where = at((x + k) % SIDE, y, c)
        part = u.at[x, :, columns(g)]
        return remote(part, part, u_send.at[g, k], u_recv.at[g, k], where)

    for g in range(2):
        for k in (2, 1, 3):
            t_out[k, :, columns(g)] = t_part(g, (x + k) % SIDE).astype(bf16)
            t_copy(g, k).start()
    for g in range(2):
        t_sum[:, columns(g)] = t_part(g, x)
    gram_t[...] = (
        gram[:, :, 0:PART].reshape(BLOCK, BLOCK).T.reshape(SIDE, ROWS, BLOCK)
    )
    for g in range(2):
        part = columns(g)
        for k in (1, 3, 2):
            t_copy(g, k).wait_recv()
            t_sum[:, part] += t_in[k, :, part].astype(f32)
        u[x, :, part] = (
            coef_quad * xj[x, :, part].astype(f32) + coef_cubic * t_sum[:, part]
        ).astype(bf16)
        for k in (2, 1, 3):
            u_copy(g, k).start()

    def p_copy(g, q):
        part = columns(g)
        return remote(
            p_out.at[q, :, part], p_in.at[y, :, part], p_send.at[g, q], p_recv.at[g, y], from_i(q)
        )

    for g in range(2):
        part = columns(g)
        for k in (1, 3, 2):
            arrived(u.at[(x + SIDE - k) % SIDE, :, part], u_recv.at[g, k])
        right = u[:, :, part].reshape(BLOCK, GROUPS[g][1])
        for q in range(SIDE):
            local = jnp.logical_and(own, q == quarter)
            p_out[q, :, part] = jnp.dot(gram_t[q], right, preferred_element_type=f32).astype(bf16)

            @pl.when(local)
            def _():
                pltpu.make_async_copy(
                    p_out.at[q, :, part], p_in.at[y, :, part], p_recv.at[g, y]
                ).start()

            @pl.when(jnp.logical_not(local))
            def _():
                p_copy(g, q).start()

    finish()
    for g in range(2):
        part = columns(g)
        result = coef_linear * m_ref[:, part].astype(f32)
        for k in range(SIDE):
            arrived(p_in.at[k, :, part], p_recv.at[g, k])
            result += p_in[k, :, part].astype(f32)
        out_ref[:, part] = (result * math.sqrt(max(M, N))).astype(bf16)
    for g in range(2):
        for q in range(SIDE):

            @pl.when(jnp.logical_not(jnp.logical_and(own, q == quarter)))
            def _():
                p_copy(g, q).wait_send()


def body(momentum, stop=0):
    bf16, f32 = jnp.bfloat16, jnp.float32
    block = (SIDE, ROWS, COLS)
    sem = pltpu.SemaphoreType.DMA
    return pl.pallas_call(
        functools.partial(kernel, stop),
        out_shape=jax.ShapeDtypeStruct((ROWS, COLS), bf16),
        in_specs=[pl.BlockSpec(memory_space=pltpu.VMEM)],
        out_specs=pl.BlockSpec(memory_space=pltpu.VMEM),
        scratch_shapes=[
            pltpu.VMEM(block, bf16),
            pltpu.VMEM(block, bf16),
            pltpu.VMEM((4, PART, BLOCK), f32),
            pltpu.VMEM((4, PART, BLOCK), bf16),
            pltpu.VMEM((4, PART, BLOCK), bf16),
            pltpu.VMEM((3, PART, BLOCK), bf16),
            pltpu.VMEM((3, PART, BLOCK), bf16),
            pltpu.VMEM((PADDED, BLOCK), f32),
            pltpu.VMEM((PADDED, BLOCK), bf16),
            pltpu.VMEM((3, PIECE, BLOCK), bf16),
            pltpu.VMEM((2, 4, PADDED, BLOCK), bf16),
            pltpu.VMEM((SIDE, ROWS, BLOCK), bf16),
            pltpu.VMEM(block, bf16),
            pltpu.VMEM(block, bf16),
            pltpu.VMEM((ROWS, COLS), f32),
            pltpu.VMEM(block, bf16),
            pltpu.VMEM(block, bf16),
            pltpu.VMEM(block, bf16),
            sem((SIDE,)), sem((SIDE,)),
            sem((SIDE,)), sem((SIDE,)),
            sem((2,)), sem((2,)),
            sem((3,)), sem((3,)),
            sem((3,)), sem((3,)),
            sem((3,)), sem((3,)),
            sem((3,)), sem((3,)),
            sem((4,)), sem((4,)),
            sem((2, SIDE)), sem((2, SIDE)),
            sem((2, SIDE)), sem((2, SIDE)),
            sem((2, SIDE)), sem((2, SIDE)),
        ],
        compiler_params=pltpu.CompilerParams(
            collective_id=0, has_side_effects=True, vmem_limit_bytes=48 * 2**20
        ),
        cost_estimate=pl.CostEstimate(
            flops=6 * BLOCK * BLOCK * COLS, bytes_accessed=4 * ROWS * COLS, transcendentals=0
        ),
        name="newton_schulz",
    )(momentum)


def solution(mesh):
    return jax.shard_map(
        body,
        mesh=mesh,
        in_specs=(P("row", "col"),),
        out_specs=P("row", "col"),
        check_vma=False,
    )
```

```python
import math

import jax
import jax.numpy as jnp
from jax import lax
from jax.experimental import pallas as pl
from jax.experimental.pallas import tpu as pltpu
from jax.sharding import PartitionSpec as P

M = 3584
N = 18432

coef_linear = 3.4445
coef_quad = -4.775
coef_cubic = 2.0315

SIDE = 4
DEPTH = 16
BLOCK = M // SIDE
ROWS = BLOCK // SIDE
COLS = N // 32
PART = ROWS // 2
PIECE = 32
PADDED = 4 * PIECE
HALVES = ((0, 512), (512, BLOCK - 512))
SHARES = ((0, 128), (128, ROWS - 128))
FIRST = pl.ds(0, 256)
SECOND = pl.ds(256, COLS - 256)
NT = (((1,), (1,)), ((), ()))


def kernel(
    m_ref, out_ref, swap, xi, xj, acc, sib_out, sib_in, near_out, near_in, cls, far_out, far_in,
    gram, gram_t, tx_out, tx_in, tx_sum, ty_out, ty_in, ux, uy, px_out, px_in, py_out, py_in,
    fin_out, fin_in,
    i_send, i_recv, j_send, j_recv, s_send, s_recv, near_send, near_recv, far_send, far_recv,
    gf_send, gf_recv, gn_send, gn_recv, h_send, h_recv, w_send, w_recv,
    tx_send, tx_recv, ty_send, ty_recv, ux_send, ux_recv, uy_send, uy_recv,
    px_send, px_recv, py_send, py_recv, fin_send, fin_recv,
):
    row, col = lax.axis_index("row"), lax.axis_index("col")
    x, y_lo, c = row // 4, (row // 2) % 2, row % 2
    z, y_hi = col // 2, col % 2
    y = y_hi * 2 + y_lo
    quarter = y_lo * 2 + c
    r, a = z % 4, z // 4
    bf16, f32 = jnp.bfloat16, jnp.float32

    def at(x_, y_, c_):
        return ((x_ * 2 + y_ % 2) * 2 + c_, z * 2 + y_ // 2)

    def along(d):
        return (row, ((z + d + DEPTH) % DEPTH) * 2 + y_hi)

    def remote(src, dst, send, recv, where):
        return pltpu.make_async_remote_copy(
            src_ref=src, dst_ref=dst, send_sem=send, recv_sem=recv,
            device_id=where, device_id_type=pl.DeviceIdType.MESH,
        )

    def arrived(dst, recv):
        pltpu.make_async_copy(dst, dst, recv).wait()

    def to_i(k):
        return at(x, k, y_hi)

    def from_i(k):
        return at(x, c * 2 + k // 2, k % 2)

    def on_x(k):
        return at((x + k) % SIDE, y, c)

    def on_y(k):
        return at(x, (y + k) % SIDE, c)

    sibling = at(x, y, 1 - c)
    peer = at(x, (y + 2) % SIDE, 1 - c)
    own = c == y_hi
    others = jnp.logical_not(own)
    near = (1, -1, 2 - 4 * c)

    barrier = pltpu.get_barrier_semaphore()

    def signal(where):
        pl.semaphore_signal(barrier, inc=1, device_id=where, device_id_type=pl.DeviceIdType.MESH)

    for d in (8, 4, -4, 2, -2, 1, -1):
        signal(along(d))
    for k in (2, 1, 3):
        signal(on_x(k))
        signal(on_y(k))
    for k in range(SIDE):

        @pl.when(jnp.logical_not(jnp.logical_and(own, y == k)))
        def _():
            signal(to_i(k))

        @pl.when(jnp.logical_not(jnp.logical_and(own, quarter == k)))
        def _():
            signal(from_i(k))

    signal(peer)
    signal(sibling)
    pl.semaphore_wait(barrier, 23 - 2 * own.astype(jnp.int32))

    def block(ref, k):
        return ref.at[pl.ds(pl.multiple_of(k * ROWS, ROWS), ROWS)]

    common = y_lo * 2 + y_hi
    handed = y_lo * 2 + 1 - y_hi
    swap_copy = remote(m_ref, swap, w_send.at[0], w_recv.at[0], peer)

    def hand_i(src):
        return remote(src, block(xi, handed), i_send.at[0], i_recv.at[handed], sibling)

    def i_copy(k):
        there = block(xi, quarter)
        return remote(m_ref, there, i_send.at[k], i_recv.at[quarter], to_i((y + k) % SIDE))

    def j_copy(src, k):
        return remote(src, block(xj, x), j_send.at[k], j_recv.at[k], on_x(k))

    def keep(src):
        common_rows = pl.ds(pl.multiple_of(common * ROWS, ROWS), ROWS)
        xi[common_rows] = src[...]
        x_rows = pl.ds(pl.multiple_of(x * ROWS, ROWS), ROWS)
        xj[x_rows] = src[...]

    swap_copy.start()

    @pl.when(own)
    def _():
        for k in (2, 1, 3):
            j_copy(m_ref, k).start()
        keep(m_ref)

    @pl.when(others)
    def _():
        hand_i(m_ref).start()

    swap_copy.wait_recv()

    @pl.when(own)
    def _():
        hand_i(swap).start()

    @pl.when(others)
    def _():
        for k in (2, 1, 3):
            j_copy(swap, k).start()

    for k in (1, 3):
        i_copy(k).start()

    @pl.when(others)
    def _():
        keep(swap)

    arrived(block(xi, handed), i_recv.at[handed])
    for k in range(2):
        far_slot = (1 - y_lo) * 2 + k
        arrived(block(xi, far_slot), i_recv.at[far_slot])
    for k in (1, 2, 3):
        arrived(block(xj, (x + SIDE - k) % SIDE), j_recv.at[k])

    def half(g):
        return pl.ds(*HALVES[g])

    def s_copy(g):
        return remote(
            sib_out.at[:, :, half(g)], sib_in.at[:, :, half(g)], s_send.at[g], s_recv.at[g], sibling
        )

    def terms(core, g):
        rows = pl.ds(pl.multiple_of(core * (BLOCK // 2), BLOCK // 2), BLOCK // 2)
        return lax.dot_general(xi[rows], xj[half(g)], NT, preferred_element_type=f32).reshape(
            4, PART, HALVES[g][1]
        )

    for g in range(2):
        sib_out[:, :, half(g)] = terms(1 - c, g).astype(bf16)
        s_copy(g).start()
        acc[:, :, half(g)] = terms(c, g)

    def near_copy(g, k):
        return remote(
            near_out.at[k, :, half(g)], near_in.at[k, :, half(g)],
            near_send.at[g, k], near_recv.at[g, k], along(near[k]),
        )

    def far_copy(g, k):
        piece = pl.ds(pl.multiple_of(((a + k + 1) % 4) * PIECE, PIECE), PIECE)
        return remote(
            far_out.at[piece, half(g)], far_in.at[k, :, half(g)],
            far_send.at[g, k], far_recv.at[g, k], along(4 * (k + 1)),
        )

    def mine(k=0):
        return pl.ds(pl.multiple_of(((a + 4 - k) % 4) * PIECE, PIECE), PIECE)

    def gf_copy(g, k):
        piece = gram.at[c, r, mine(), half(g)]
        return remote(piece, piece, gf_send.at[g, k], gf_recv.at[g, k], along(4 * (k + 1)))

    def quarter_of(core, q, g):
        return gram.at[core, q, pl.ds(0, PART), half(g)]

    def gn_copy(g, k):
        part = quarter_of(c, r, g)
        return remote(part, part, gn_send.at[g, k], gn_recv.at[g, k], along(near[k]))

    def hand(g, k):
        part = quarter_of(c, (r + k) % 4, g)
        return remote(part, part, h_send.at[g, k], h_recv.at[g, k], sibling)

    cls[PART:] = jnp.zeros_like(cls[PART:])
    for g in range(2):
        s_copy(g).wait_recv()
        for k in (2, 0, 1):
            q = (r + near[k] + 4) % 4
            near_out[k, :, half(g)] = (
                acc[q, :, half(g)] + sib_in[q, :, half(g)].astype(f32)
            ).astype(bf16)
            near_copy(g, k).start()
        cls[0:PART, half(g)] = acc[r, :, half(g)] + sib_in[r, :, half(g)].astype(f32)
    for g in range(2):
        for k in (0, 1, 2):
            near_copy(g, k).wait_recv()
        cls[0:PART, half(g)] += (
            near_in[0, :, half(g)].astype(f32)
            + near_in[1, :, half(g)].astype(f32)
            + near_in[2, :, half(g)].astype(f32)
        )
        far_out[:, half(g)] = cls[:, half(g)].astype(bf16)
        for k in (1, 0, 2):
            far_copy(g, k).start()

    for g in range(2):
        total = cls[mine(), half(g)]
        for k in (0, 2, 1):
            far_copy(g, k).wait_recv()
            total += far_in[k, :, half(g)].astype(f32)
        gram[c, r, mine(), half(g)] = total.astype(bf16)
        for k in (1, 0, 2):
            gf_copy(g, k).start()
    for g in range(2):
        for k in (0, 2, 1):
            arrived(gram.at[c, r, mine(k + 1), half(g)], gf_recv.at[g, k])
        for k in (2, 0, 1):
            gn_copy(g, k).start()
        hand(g, 0).start()

    def share(g):
        return pl.ds(*SHARES[g])

    def rows_of(g, q):
        first, size = HALVES[g][0], SHARES[g][1]
        return pl.ds(pl.multiple_of(first + q * size, PIECE), size)

    def rows_at(q):
        return pl.ds(pl.multiple_of(q * ROWS, ROWS), ROWS)

    def gram_rows(q):
        return gram[q // 2, pl.ds((q % 2) * 2, 2), 0:PART].reshape(ROWS, BLOCK)

    def dot(left, right):
        return jnp.dot(left, right, preferred_element_type=f32)

    def tx_copy(g, k):
        return remote(
            tx_out.at[k, share(g)], tx_in.at[k, share(g)],
            tx_send.at[g, k], tx_recv.at[g, k], on_x(k),
        )

    def ty_copy(k):
        return remote(ty_out.at[k], ty_in.at[k], ty_send.at[k], ty_recv.at[k], on_y(k))

    for g in range(2):
        for k in (0, 1, 2):
            arrived(quarter_of(c, (r - near[k] + 4) % 4, g), gn_recv.at[g, k])
            hand(g, (3, 1, 2)[k]).start()
        for k in (0, 3, 1, 2):
            arrived(quarter_of(1 - c, (r + k) % 4, g), h_recv.at[g, k])
        if g == 1:
            for k in (2, 1, 3):
                ty_out[k] = dot(gram_rows((y + k) % SIDE), xj[:, FIRST]).astype(bf16)
                ty_copy(k).start()
        gram_t[half(g)] = gram[:, :, 0:PART, half(g)].reshape(BLOCK, HALVES[g][1]).T
        for k in (2, 1, 3):
            tx_out[k, share(g)] = dot(gram_t[rows_of(g, (x + k) % SIDE)], xi[:, SECOND]).astype(
                bf16
            )
            tx_copy(g, k).start()
        tx_sum[share(g)] = dot(gram_t[rows_of(g, x)], xi[:, SECOND])

    def ux_copy(g, k):
        here = ux.at[rows_of(g, x)]
        return remote(here, here, ux_send.at[g, k], ux_recv.at[g, k], on_x(k))

    def uy_copy(k):
        here = uy.at[rows_at(y)]
        return remote(here, here, uy_send.at[k], uy_recv.at[k], on_y(k))

    def ux_part(g):
        total = tx_sum[share(g)]
        for k in (1, 3, 2):
            tx_copy(g, k).wait_recv()
            total += tx_in[k, share(g)].astype(f32)
        ux[rows_of(g, x)] = (
            coef_quad * xj[rows_of(g, x), SECOND].astype(f32) + coef_cubic * total
        ).astype(bf16)
        for k in (2, 1, 3):
            ux_copy(g, k).start()

    ux_part(0)
    total = dot(gram_rows(y), xj[:, FIRST])
    for k in (1, 3, 2):
        ty_copy(k).wait_recv()
        total += ty_in[k].astype(f32)
    uy[rows_at(y)] = (
        coef_quad * xi[rows_at(y), FIRST].astype(f32) + coef_cubic * total
    ).astype(bf16)
    for k in (2, 1, 3):
        uy_copy(k).start()
    ux_part(1)

    def px_copy(k):
        return remote(px_out.at[k], px_in.at[k], px_send.at[k], px_recv.at[k], on_x(k))

    def py_copy(q):
        return remote(py_out.at[q], py_in.at[y], py_send.at[q], py_recv.at[y], from_i(q))

    for k in (1, 3, 2):
        arrived(uy.at[rows_at((y + SIDE - k) % SIDE)], uy_recv.at[k])
    for k in (2, 1, 3):
        px_out[k] = dot(gram_t[rows_at((x + k) % SIDE)], uy[...]).astype(bf16)
        px_copy(k).start()
    for g in range(2):
        for k in (1, 3, 2):
            arrived(ux.at[rows_of(g, (x + SIDE - k) % SIDE)], ux_recv.at[g, k])
    for q in range(SIDE):
        local = jnp.logical_and(own, q == quarter)
        py_out[q] = dot(gram_rows(q), ux[...]).astype(bf16)

        @pl.when(local)
        def _():
            pltpu.make_async_copy(py_out.at[q], py_in.at[y], py_recv.at[y]).start()

        @pl.when(jnp.logical_not(local))
        def _():
            py_copy(q).start()

    factor = math.sqrt(max(M, N))
    total = dot(gram_t[rows_at(x)], uy[...])
    total += coef_linear * xj[rows_at(x), FIRST].astype(f32)
    for k in (1, 3, 2):
        px_copy(k).wait_recv()
        total += px_in[k].astype(f32)
    fin_out[...] = (total * factor).astype(bf16)
    fin_copy = remote(fin_out, fin_in, fin_send.at[0], fin_recv.at[0], peer)

    @pl.when(own)
    def _():
        out_ref[:, FIRST] = fin_out[...]

    @pl.when(others)
    def _():
        fin_copy.start()

    swap_copy.wait_send()
    hand_i(m_ref).wait_send()
    for k in (1, 3):
        i_copy(k).wait_send()
    for k in (1, 2, 3):
        j_copy(m_ref, k).wait_send()
    for g in range(2):
        s_copy(g).wait_send()
        for k in range(3):
            near_copy(g, k).wait_send()
            far_copy(g, k).wait_send()
            gf_copy(g, k).wait_send()
            gn_copy(g, k).wait_send()
        for k in range(4):
            hand(g, k).wait_send()
        for k in (1, 2, 3):
            tx_copy(g, k).wait_send()
            ux_copy(g, k).wait_send()
    for k in (1, 2, 3):
        ty_copy(k).wait_send()
        uy_copy(k).wait_send()
        px_copy(k).wait_send()

    result = coef_linear * m_ref[:, SECOND].astype(f32)
    for k in range(SIDE):
        arrived(py_in.at[k], py_recv.at[k])
        result += py_in[k].astype(f32)
    out_ref[:, SECOND] = (result * factor).astype(bf16)

    @pl.when(others)
    def _():
        fin_copy.wait_recv()
        out_ref[:, FIRST] = fin_in[...]
        fin_copy.wait_send()

    for q in range(SIDE):

        @pl.when(jnp.logical_not(jnp.logical_and(own, q == quarter)))
        def _():
            py_copy(q).wait_send()


def body(momentum):
    bf16, f32 = jnp.bfloat16, jnp.float32
    first = (SIDE, ROWS, FIRST.size)
    second = (SIDE, ROWS, SECOND.size)
    sem = pltpu.SemaphoreType.DMA
    return pl.pallas_call(
        kernel,
        out_shape=jax.ShapeDtypeStruct((ROWS, COLS), bf16),
        in_specs=[pl.BlockSpec(memory_space=pltpu.VMEM)],
        out_specs=pl.BlockSpec(memory_space=pltpu.VMEM),
        scratch_shapes=[
            pltpu.VMEM((ROWS, COLS), bf16),
            pltpu.VMEM((BLOCK, COLS), bf16),
            pltpu.VMEM((BLOCK, COLS), bf16),
            pltpu.VMEM((4, PART, BLOCK), f32),
            pltpu.VMEM((4, PART, BLOCK), bf16),
            pltpu.VMEM((4, PART, BLOCK), bf16),
            pltpu.VMEM((3, PART, BLOCK), bf16),
            pltpu.VMEM((3, PART, BLOCK), bf16),
            pltpu.VMEM((PADDED, BLOCK), f32),
            pltpu.VMEM((PADDED, BLOCK), bf16),
            pltpu.VMEM((3, PIECE, BLOCK), bf16),
            pltpu.VMEM((2, 4, PADDED, BLOCK), bf16),
            pltpu.VMEM((BLOCK, BLOCK), bf16),
            pltpu.VMEM(second, bf16),
            pltpu.VMEM(second, bf16),
            pltpu.VMEM(second[1:], f32),
            pltpu.VMEM(first, bf16),
            pltpu.VMEM(first, bf16),
            pltpu.VMEM((BLOCK, SECOND.size), bf16),
            pltpu.VMEM((BLOCK, FIRST.size), bf16),
            pltpu.VMEM(first, bf16),
            pltpu.VMEM(first, bf16),
            pltpu.VMEM(second, bf16),
            pltpu.VMEM(second, bf16),
            pltpu.VMEM(first[1:], bf16),
            pltpu.VMEM(first[1:], bf16),
            sem((SIDE,)), sem((SIDE,)),
            sem((SIDE,)), sem((SIDE,)),
            sem((2,)), sem((2,)),
            sem((2, 3)), sem((2, 3)),
            sem((2, 3)), sem((2, 3)),
            sem((2, 3)), sem((2, 3)),
            sem((2, 3)), sem((2, 3)),
            sem((2, 4)), sem((2, 4)),
            sem((1,)), sem((1,)),
            sem((2, SIDE)), sem((2, SIDE)),
            sem((SIDE,)), sem((SIDE,)),
            sem((2, SIDE)), sem((2, SIDE)),
            sem((SIDE,)), sem((SIDE,)),
            sem((SIDE,)), sem((SIDE,)),
            sem((SIDE,)), sem((SIDE,)),
            sem((1,)), sem((1,)),
        ],
        compiler_params=pltpu.CompilerParams(
            collective_id=0, has_side_effects=True, vmem_limit_bytes=48 * 2**20
        ),
        cost_estimate=pl.CostEstimate(
            flops=6 * BLOCK * BLOCK * COLS, bytes_accessed=4 * ROWS * COLS, transcendentals=0
        ),
        name="newton_schulz",
    )(momentum)


def solution(mesh):
    return jax.shard_map(
        body,
        mesh=mesh,
        in_specs=(P("row", "col"),),
        out_specs=P("row", "col"),
        check_vma=False,
    )
```

```python
import math

import jax
import jax.numpy as jnp
from jax import lax
from jax.experimental import pallas as pl
from jax.experimental.pallas import tpu as pltpu
from jax.sharding import PartitionSpec as P

M = 3584
N = 18432

coef_linear = 3.4445
coef_quad = -4.775
coef_cubic = 2.0315

SIDE = 4
DEPTH = 16
BLOCK = M // SIDE
ROWS = BLOCK // SIDE
COLS = N // 32
PART = ROWS // 2
PIECE = 32
PADDED = 4 * PIECE
HALVES = ((0, 512), (512, BLOCK - 512))
SHARES = ((0, 128), (128, ROWS - 128))
FIRST = pl.ds(0, 256)
STRIP = 128
SECOND = pl.ds(256, COLS - 256)
NT = (((1,), (1,)), ((), ()))


def kernel(
    m_ref, out_ref, swap, xi, xj, acc, sib_out, sib_in, near_out, near_in, cls, far_out, far_in,
    gram, gram_t, tx_out, tx_in, tx_sum, ty_out, ty_in, ux, uy, px_out, px_in, py_out, py_in,
    fin_out, fin_in,
    i_send, i_recv, j_send, j_recv, s_send, s_recv, near_send, near_recv, far_send, far_recv,
    gf_send, gf_recv, gn_send, gn_recv, h_send, h_recv, w_send, w_recv,
    tx_send, tx_recv, ty_send, ty_recv, ux_send, ux_recv, uy_send, uy_recv,
    px_send, px_recv, py_send, py_recv, fin_send, fin_recv, inside,
):
    row, col = lax.axis_index("row"), lax.axis_index("col")
    x, y_lo, c = row // 4, (row // 2) % 2, row % 2
    z, y_hi = col // 2, col % 2
    y = y_hi * 2 + y_lo
    quarter = y_lo * 2 + c
    r, a = z % 4, z // 4
    bf16, f32 = jnp.bfloat16, jnp.float32

    def at(x_, y_, c_):
        return ((x_ * 2 + y_ % 2) * 2 + c_, z * 2 + y_ // 2)

    def along(d):
        return (row, ((z + d + DEPTH) % DEPTH) * 2 + y_hi)

    def remote(src, dst, send, recv, where):
        return pltpu.make_async_remote_copy(
            src_ref=src, dst_ref=dst, send_sem=send, recv_sem=recv,
            device_id=where, device_id_type=pl.DeviceIdType.MESH,
        )

    def arrived(dst, recv):
        pltpu.make_async_copy(dst, dst, recv).wait()

    def to_i(k):
        return at(x, k, y_hi)

    def from_i(k):
        return at(x, c * 2 + k // 2, k % 2)

    def on_x(k):
        return at((x + k) % SIDE, y, c)

    def on_y(k):
        return at(x, (y + k) % SIDE, c)

    sibling = at(x, y, 1 - c)
    peer = at(x, (y + 2) % SIDE, 1 - c)
    own = c == y_hi
    others = jnp.logical_not(own)
    near = (1, -1, 2 - 4 * c)

    barrier = pltpu.get_barrier_semaphore()

    def signal(where):
        pl.semaphore_signal(barrier, inc=1, device_id=where, device_id_type=pl.DeviceIdType.MESH)

    for d in (2, -2, 1, -1):
        signal(along(d))
    for k in (2, 1, 3):
        signal(on_x(k))
        signal(on_y(k))
    for k in range(SIDE):

        @pl.when(jnp.logical_not(jnp.logical_and(own, y == k)))
        def _():
            signal(to_i(k))

        @pl.when(jnp.logical_not(jnp.logical_and(own, quarter == k)))
        def _():
            signal(from_i(k))

    signal(peer)
    signal(sibling)
    pl.semaphore_wait(barrier, 20 - 2 * own.astype(jnp.int32))

    def pass_on(k, d):
        for e in (d, -d):
            pl.semaphore_signal(
                inside.at[k], inc=1, device_id=along(e), device_id_type=pl.DeviceIdType.MESH
            )

    pass_on(0, 2)

    def block(ref, k):
        return ref.at[pl.ds(pl.multiple_of(k * ROWS, ROWS), ROWS)]

    common = y_lo * 2 + y_hi
    handed = y_lo * 2 + 1 - y_hi
    swap_copy = remote(m_ref, swap, w_send.at[0], w_recv.at[0], peer)

    def hand_i(src):
        return remote(src, block(xi, handed), i_send.at[0], i_recv.at[handed], sibling)

    def i_copy(k):
        there = block(xi, quarter)
        return remote(m_ref, there, i_send.at[k], i_recv.at[quarter], to_i((y + k) % SIDE))

    def j_copy(src, k):
        return remote(src, block(xj, x), j_send.at[k], j_recv.at[k], on_x(k))

    def keep(src):
        common_rows = pl.ds(pl.multiple_of(common * ROWS, ROWS), ROWS)
        xi[common_rows] = src[...]
        x_rows = pl.ds(pl.multiple_of(x * ROWS, ROWS), ROWS)
        xj[x_rows] = src[...]

    swap_copy.start()

    @pl.when(own)
    def _():
        for k in (2, 1, 3):
            j_copy(m_ref, k).start()
        keep(m_ref)

    @pl.when(others)
    def _():
        hand_i(m_ref).start()

    swap_copy.wait_recv()

    @pl.when(own)
    def _():
        hand_i(swap).start()

    @pl.when(others)
    def _():
        for k in (2, 1, 3):
            j_copy(swap, k).start()

    for k in (1, 3):
        i_copy(k).start()

    @pl.when(others)
    def _():
        keep(swap)

    arrived(block(xi, handed), i_recv.at[handed])
    for k in range(2):
        far_slot = (1 - y_lo) * 2 + k
        arrived(block(xi, far_slot), i_recv.at[far_slot])
    for k in (1, 2, 3):
        arrived(block(xj, (x + SIDE - k) % SIDE), j_recv.at[k])

    pl.semaphore_wait(inside.at[0], 2)
    pass_on(1, 4)

    def half(g):
        return pl.ds(*HALVES[g])

    def s_copy(g):
        return remote(
            sib_out.at[:, :, half(g)], sib_in.at[:, :, half(g)], s_send.at[g], s_recv.at[g], sibling
        )

    def terms(core, g):
        rows = pl.ds(pl.multiple_of(core * (BLOCK // 2), BLOCK // 2), BLOCK // 2)
        return lax.dot_general(xi[rows], xj[half(g)], NT, preferred_element_type=f32).reshape(
            4, PART, HALVES[g][1]
        )

    for g in range(2):
        sib_out[:, :, half(g)] = terms(1 - c, g).astype(bf16)
        s_copy(g).start()
        acc[:, :, half(g)] = terms(c, g)

    def near_copy(g, k):
        return remote(
            near_out.at[k, :, half(g)], near_in.at[k, :, half(g)],
            near_send.at[g, k], near_recv.at[g, k], along(near[k]),
        )

    def far_copy(g, k):
        piece = pl.ds(pl.multiple_of(((a + k + 1) % 4) * PIECE, PIECE), PIECE)
        return remote(
            far_out.at[piece, half(g)], far_in.at[k, :, half(g)],
            far_send.at[g, k], far_recv.at[g, k], along(4 * (k + 1)),
        )

    def mine(k=0):
        return pl.ds(pl.multiple_of(((a + 4 - k) % 4) * PIECE, PIECE), PIECE)

    def gf_copy(g, k):
        piece = gram.at[c, r, mine(), half(g)]
        return remote(piece, piece, gf_send.at[g, k], gf_recv.at[g, k], along(4 * (k + 1)))

    def quarter_of(core, q, g):
        return gram.at[core, q, pl.ds(0, PART), half(g)]

    def gn_copy(g, k):
        part = quarter_of(c, r, g)
        return remote(part, part, gn_send.at[g, k], gn_recv.at[g, k], along(near[k]))

    def hand(g, k):
        part = quarter_of(c, (r + k) % 4, g)
        return remote(part, part, h_send.at[g, k], h_recv.at[g, k], sibling)

    cls[PART:] = jnp.zeros_like(cls[PART:])
    for g in range(2):
        s_copy(g).wait_recv()
        for k in (2, 0, 1):
            q = (r + near[k] + 4) % 4
            near_out[k, :, half(g)] = (
                acc[q, :, half(g)] + sib_in[q, :, half(g)].astype(f32)
            ).astype(bf16)
            near_copy(g, k).start()
        cls[0:PART, half(g)] = acc[r, :, half(g)] + sib_in[r, :, half(g)].astype(f32)
    pl.semaphore_wait(inside.at[1], 2)
    for g in range(2):
        for k in (0, 1, 2):
            near_copy(g, k).wait_recv()
        cls[0:PART, half(g)] += (
            near_in[0, :, half(g)].astype(f32)
            + near_in[1, :, half(g)].astype(f32)
            + near_in[2, :, half(g)].astype(f32)
        )
        far_out[:, half(g)] = cls[:, half(g)].astype(bf16)
        for k in (1, 0, 2):
            far_copy(g, k).start()

    for g in range(2):
        total = cls[mine(), half(g)]
        for k in (0, 2, 1):
            far_copy(g, k).wait_recv()
            total += far_in[k, :, half(g)].astype(f32)
        gram[c, r, mine(), half(g)] = total.astype(bf16)
        for k in (1, 0, 2):
            gf_copy(g, k).start()
    for g in range(2):
        for k in (0, 2, 1):
            arrived(gram.at[c, r, mine(k + 1), half(g)], gf_recv.at[g, k])
        for k in (2, 0, 1):
            gn_copy(g, k).start()
        hand(g, 0).start()

    def share(g):
        return pl.ds(*SHARES[g])

    def rows_of(g, q):
        first, size = HALVES[g][0], SHARES[g][1]
        return pl.ds(pl.multiple_of(first + q * size, PIECE), size)

    def rows_at(q):
        return pl.ds(pl.multiple_of(q * ROWS, ROWS), ROWS)

    def gram_rows(q):
        return gram[q // 2, pl.ds((q % 2) * 2, 2), 0:PART].reshape(ROWS, BLOCK)

    def dot(left, right):
        return jnp.dot(left, right, preferred_element_type=f32)

    def tx_copy(g, k):
        return remote(
            tx_out.at[k, share(g)], tx_in.at[k, share(g)],
            tx_send.at[g, k], tx_recv.at[g, k], on_x(k),
        )

    def strip(f):
        return pl.ds(f * STRIP, STRIP)

    def ty_copy(f, k):
        return remote(
            ty_out.at[k, :, strip(f)], ty_in.at[k, :, strip(f)],
            ty_send.at[f, k], ty_recv.at[f, k], on_y(k),
        )

    for g in range(2):
        for k in (0, 1, 2):
            arrived(quarter_of(c, (r - near[k] + 4) % 4, g), gn_recv.at[g, k])
            hand(g, (3, 1, 2)[k]).start()
        for k in (0, 3, 1, 2):
            arrived(quarter_of(1 - c, (r + k) % 4, g), h_recv.at[g, k])
        if g == 1:
            for f in range(2):
                for k in (2, 1, 3):
                    ty_out[k, :, strip(f)] = dot(
                        gram_rows((y + k) % SIDE), xj[:, strip(f)]
                    ).astype(bf16)
                    ty_copy(f, k).start()
        gram_t[half(g)] = gram[:, :, 0:PART, half(g)].reshape(BLOCK, HALVES[g][1]).T
        for k in (2, 1, 3):
            tx_out[k, share(g)] = dot(gram_t[rows_of(g, (x + k) % SIDE)], xi[:, SECOND]).astype(
                bf16
            )
            tx_copy(g, k).start()
        tx_sum[share(g)] = dot(gram_t[rows_of(g, x)], xi[:, SECOND])

    def ux_copy(g, k):
        here = ux.at[rows_of(g, x)]
        return remote(here, here, ux_send.at[g, k], ux_recv.at[g, k], on_x(k))

    def uy_copy(f, k):
        here = uy.at[rows_at(y), strip(f)]
        return remote(here, here, uy_send.at[f, k], uy_recv.at[f, k], on_y(k))

    def ux_part(g):
        total = tx_sum[share(g)]
        for k in (1, 3, 2):
            tx_copy(g, k).wait_recv()
            total += tx_in[k, share(g)].astype(f32)
        ux[rows_of(g, x)] = (
            coef_quad * xj[rows_of(g, x), SECOND].astype(f32) + coef_cubic * total
        ).astype(bf16)
        for k in (2, 1, 3):
            ux_copy(g, k).start()

    ux_part(0)
    for f in range(2):
        total = dot(gram_rows(y), xj[:, strip(f)])
        for k in (1, 3, 2):
            ty_copy(f, k).wait_recv()
            total += ty_in[k, :, strip(f)].astype(f32)
        uy[rows_at(y), strip(f)] = (
            coef_quad * xi[rows_at(y), strip(f)].astype(f32) + coef_cubic * total
        ).astype(bf16)
        for k in (2, 1, 3):
            uy_copy(f, k).start()
    ux_part(1)

    def px_copy(f, k):
        return remote(
            px_out.at[k, :, strip(f)], px_in.at[k, :, strip(f)],
            px_send.at[f, k], px_recv.at[f, k], on_x(k),
        )

    def py_copy(q):
        return remote(py_out.at[q], py_in.at[y], py_send.at[q], py_recv.at[y], from_i(q))

    for f in range(2):
        for k in (1, 3, 2):
            arrived(uy.at[rows_at((y + SIDE - k) % SIDE), strip(f)], uy_recv.at[f, k])
        for k in (2, 1, 3):
            px_out[k, :, strip(f)] = dot(
                gram_t[rows_at((x + k) % SIDE)], uy[:, strip(f)]
            ).astype(bf16)
            px_copy(f, k).start()
    for g in range(2):
        for k in (1, 3, 2):
            arrived(ux.at[rows_of(g, (x + SIDE - k) % SIDE)], ux_recv.at[g, k])
    for q in range(SIDE):
        local = jnp.logical_and(own, q == quarter)
        py_out[q] = dot(gram_rows(q), ux[...]).astype(bf16)

        @pl.when(local)
        def _():
            pltpu.make_async_copy(py_out.at[q], py_in.at[y], py_recv.at[y]).start()

        @pl.when(jnp.logical_not(local))
        def _():
            py_copy(q).start()

    factor = math.sqrt(max(M, N))

    def fin_copy(f):
        part = strip(f)
        return remote(
            fin_out.at[:, part], fin_in.at[:, part], fin_send.at[f], fin_recv.at[f], peer
        )

    for f in range(2):
        total = dot(gram_t[rows_at(x)], uy[:, strip(f)])
        total += coef_linear * xj[rows_at(x), strip(f)].astype(f32)
        for k in (1, 3, 2):
            px_copy(f, k).wait_recv()
            total += px_in[k, :, strip(f)].astype(f32)
        fin_out[:, strip(f)] = (total * factor).astype(bf16)

        @pl.when(others)
        def _():
            fin_copy(f).start()

    @pl.when(own)
    def _():
        out_ref[:, FIRST] = fin_out[...]

    swap_copy.wait_send()
    hand_i(m_ref).wait_send()
    for k in (1, 3):
        i_copy(k).wait_send()
    for k in (1, 2, 3):
        j_copy(m_ref, k).wait_send()
    for g in range(2):
        s_copy(g).wait_send()
        for k in range(3):
            near_copy(g, k).wait_send()
            far_copy(g, k).wait_send()
            gf_copy(g, k).wait_send()
            gn_copy(g, k).wait_send()
        for k in range(4):
            hand(g, k).wait_send()
        for k in (1, 2, 3):
            tx_copy(g, k).wait_send()
            ux_copy(g, k).wait_send()
    for f in range(2):
        for k in (1, 2, 3):
            ty_copy(f, k).wait_send()
            uy_copy(f, k).wait_send()
            px_copy(f, k).wait_send()

    result = coef_linear * m_ref[:, SECOND].astype(f32)
    for k in range(SIDE):
        arrived(py_in.at[k], py_recv.at[k])
        result += py_in[k].astype(f32)
    out_ref[:, SECOND] = (result * factor).astype(bf16)

    @pl.when(others)
    def _():
        for f in range(2):
            fin_copy(f).wait_recv()
            out_ref[:, strip(f)] = fin_in[:, strip(f)]
            fin_copy(f).wait_send()

    for q in range(SIDE):

        @pl.when(jnp.logical_not(jnp.logical_and(own, q == quarter)))
        def _():
            py_copy(q).wait_send()


def body(momentum):
    bf16, f32 = jnp.bfloat16, jnp.float32
    first = (SIDE, ROWS, FIRST.size)
    second = (SIDE, ROWS, SECOND.size)
    sem = pltpu.SemaphoreType.DMA
    return pl.pallas_call(
        kernel,
        out_shape=jax.ShapeDtypeStruct((ROWS, COLS), bf16),
        in_specs=[pl.BlockSpec(memory_space=pltpu.VMEM)],
        out_specs=pl.BlockSpec(memory_space=pltpu.VMEM),
        scratch_shapes=[
            pltpu.VMEM((ROWS, COLS), bf16),
            pltpu.VMEM((BLOCK, COLS), bf16),
            pltpu.VMEM((BLOCK, COLS), bf16),
            pltpu.VMEM((4, PART, BLOCK), f32),
            pltpu.VMEM((4, PART, BLOCK), bf16),
            pltpu.VMEM((4, PART, BLOCK), bf16),
            pltpu.VMEM((3, PART, BLOCK), bf16),
            pltpu.VMEM((3, PART, BLOCK), bf16),
            pltpu.VMEM((PADDED, BLOCK), f32),
            pltpu.VMEM((PADDED, BLOCK), bf16),
            pltpu.VMEM((3, PIECE, BLOCK), bf16),
            pltpu.VMEM((2, 4, PADDED, BLOCK), bf16),
            pltpu.VMEM((BLOCK, BLOCK), bf16),
            pltpu.VMEM(second, bf16),
            pltpu.VMEM(second, bf16),
            pltpu.VMEM(second[1:], f32),
            pltpu.VMEM(first, bf16),
            pltpu.VMEM(first, bf16),
            pltpu.VMEM((BLOCK, SECOND.size), bf16),
            pltpu.VMEM((BLOCK, FIRST.size), bf16),
            pltpu.VMEM(first, bf16),
            pltpu.VMEM(first, bf16),
            pltpu.VMEM(second, bf16),
            pltpu.VMEM(second, bf16),
            pltpu.VMEM(first[1:], bf16),
            pltpu.VMEM(first[1:], bf16),
            sem((SIDE,)), sem((SIDE,)),
            sem((SIDE,)), sem((SIDE,)),
            sem((2,)), sem((2,)),
            sem((2, 3)), sem((2, 3)),
            sem((2, 3)), sem((2, 3)),
            sem((2, 3)), sem((2, 3)),
            sem((2, 3)), sem((2, 3)),
            sem((2, 4)), sem((2, 4)),
            sem((1,)), sem((1,)),
            sem((2, SIDE)), sem((2, SIDE)),
            sem((2, SIDE)), sem((2, SIDE)),
            sem((2, SIDE)), sem((2, SIDE)),
            sem((2, SIDE)), sem((2, SIDE)),
            sem((2, SIDE)), sem((2, SIDE)),
            sem((SIDE,)), sem((SIDE,)),
            sem((2,)), sem((2,)),
            pltpu.SemaphoreType.REGULAR((2,)),
        ],
        compiler_params=pltpu.CompilerParams(
            collective_id=0, has_side_effects=True, vmem_limit_bytes=48 * 2**20
        ),
        cost_estimate=pl.CostEstimate(
            flops=6 * BLOCK * BLOCK * COLS, bytes_accessed=4 * ROWS * COLS, transcendentals=0
        ),
        name="newton_schulz",
    )(momentum)


def solution(mesh):
    return jax.shard_map(
        body,
        mesh=mesh,
        in_specs=(P("row", "col"),),
        out_specs=P("row", "col"),
        check_vma=False,
    )
```

```python
import math

import jax
import jax.numpy as jnp
from jax import lax
from jax.experimental import pallas as pl
from jax.experimental.pallas import tpu as pltpu
from jax.sharding import PartitionSpec as P

M = 3584
N = 18432

coef_linear = 3.4445
coef_quad = -4.775
coef_cubic = 2.0315

SIDE = 4
DEPTH = 16
BLOCK = M // SIDE
ROWS = BLOCK // SIDE
COLS = N // 32
PART = ROWS // 2
PIECE = 32
PADDED = 4 * PIECE
HALVES = ((0, 512), (512, BLOCK - 512))
SHARES = ((0, 128), (128, ROWS - 128))
FIRST = pl.ds(0, 256)
STRIP = 128
SECOND = pl.ds(256, COLS - 256)
SPLIT = (pl.ds(0, 128), pl.ds(128, COLS - 384))
NT = (((1,), (1,)), ((), ()))


def kernel(
    m_ref, out_ref, swap, xi, xj, acc, sib_out, sib_in, near_out, near_in, cls, far_out, far_in,
    gram, gram_t, tx_out, tx_in, tx_sum, ty_out, ty_in, ux, uy, px_out, px_in, py_out, py_in,
    fin_out, fin_in,
    i_send, i_recv, j_send, j_recv, s_send, s_recv, near_send, near_recv, far_send, far_recv,
    gf_send, gf_recv, gn_send, gn_recv, h_send, h_recv, w_send, w_recv,
    tx_send, tx_recv, ty_send, ty_recv, ux_send, ux_recv, uy_send, uy_recv,
    px_send, px_recv, py_send, py_recv, fin_send, fin_recv, inside,
):
    row, col = lax.axis_index("row"), lax.axis_index("col")
    x, y_lo, c = row // 4, (row // 2) % 2, row % 2
    z, y_hi = col // 2, col % 2
    y = y_hi * 2 + y_lo
    quarter = y_lo * 2 + c
    r, a = z % 4, z // 4
    bf16, f32 = jnp.bfloat16, jnp.float32

    def at(x_, y_, c_):
        return ((x_ * 2 + y_ % 2) * 2 + c_, z * 2 + y_ // 2)

    def along(d):
        return (row, ((z + d + DEPTH) % DEPTH) * 2 + y_hi)

    def remote(src, dst, send, recv, where):
        return pltpu.make_async_remote_copy(
            src_ref=src, dst_ref=dst, send_sem=send, recv_sem=recv,
            device_id=where, device_id_type=pl.DeviceIdType.MESH,
        )

    def arrived(dst, recv):
        pltpu.make_async_copy(dst, dst, recv).wait()

    def to_i(k):
        return at(x, k, y_hi)

    def from_i(k):
        return at(x, c * 2 + k // 2, k % 2)

    def on_x(k):
        return at((x + k) % SIDE, y, c)

    def on_y(k):
        return at(x, (y + k) % SIDE, c)

    sibling = at(x, y, 1 - c)
    peer = at(x, (y + 2) % SIDE, 1 - c)
    own = c == y_hi
    others = jnp.logical_not(own)
    near = (1, -1, 2 - 4 * c)

    barrier = pltpu.get_barrier_semaphore()

    def signal(where):
        pl.semaphore_signal(barrier, inc=1, device_id=where, device_id_type=pl.DeviceIdType.MESH)

    for d in (2, -2, 1, -1):
        signal(along(d))
    for k in (2, 1, 3):
        signal(on_x(k))
        signal(on_y(k))
    for k in range(SIDE):

        @pl.when(jnp.logical_not(jnp.logical_and(own, y == k)))
        def _():
            signal(to_i(k))

        @pl.when(jnp.logical_not(jnp.logical_and(own, quarter == k)))
        def _():
            signal(from_i(k))

    signal(peer)
    signal(sibling)
    pl.semaphore_wait(barrier, 20 - 2 * own.astype(jnp.int32))

    def pass_on(k, d):
        for e in (d, -d):
            pl.semaphore_signal(
                inside.at[k], inc=1, device_id=along(e), device_id_type=pl.DeviceIdType.MESH
            )

    pass_on(0, 2)

    def block(ref, k):
        return ref.at[pl.ds(pl.multiple_of(k * ROWS, ROWS), ROWS)]

    common = y_lo * 2 + y_hi
    handed = y_lo * 2 + 1 - y_hi
    swap_copy = remote(m_ref, swap, w_send.at[0], w_recv.at[0], peer)

    def hand_i(src):
        return remote(src, block(xi, handed), i_send.at[0], i_recv.at[handed], sibling)

    def i_copy(k):
        there = block(xi, quarter)
        return remote(m_ref, there, i_send.at[k], i_recv.at[quarter], to_i((y + k) % SIDE))

    def j_copy(src, k):
        return remote(src, block(xj, x), j_send.at[k], j_recv.at[k], on_x(k))

    def keep(src):
        common_rows = pl.ds(pl.multiple_of(common * ROWS, ROWS), ROWS)
        xi[common_rows] = src[...]
        x_rows = pl.ds(pl.multiple_of(x * ROWS, ROWS), ROWS)
        xj[x_rows] = src[...]

    swap_copy.start()

    @pl.when(own)
    def _():
        for k in (2, 1, 3):
            j_copy(m_ref, k).start()
        keep(m_ref)

    @pl.when(others)
    def _():
        hand_i(m_ref).start()

    swap_copy.wait_recv()

    @pl.when(own)
    def _():
        hand_i(swap).start()

    @pl.when(others)
    def _():
        for k in (2, 1, 3):
            j_copy(swap, k).start()

    for k in (1, 3):
        i_copy(k).start()

    @pl.when(others)
    def _():
        keep(swap)

    arrived(block(xi, handed), i_recv.at[handed])
    for k in range(2):
        far_slot = (1 - y_lo) * 2 + k
        arrived(block(xi, far_slot), i_recv.at[far_slot])
    for k in (1, 2, 3):
        arrived(block(xj, (x + SIDE - k) % SIDE), j_recv.at[k])

    pl.semaphore_wait(inside.at[0], 2)
    pass_on(1, 4)

    def half(g):
        return pl.ds(*HALVES[g])

    def s_copy(g):
        return remote(
            sib_out.at[:, :, half(g)], sib_in.at[:, :, half(g)], s_send.at[g], s_recv.at[g], sibling
        )

    def terms(core, g):
        rows = pl.ds(pl.multiple_of(core * (BLOCK // 2), BLOCK // 2), BLOCK // 2)
        return lax.dot_general(xi[rows], xj[half(g)], NT, preferred_element_type=f32).reshape(
            4, PART, HALVES[g][1]
        )

    for g in range(2):
        sib_out[:, :, half(g)] = terms(1 - c, g).astype(bf16)
        s_copy(g).start()
        acc[:, :, half(g)] = terms(c, g)

    def near_copy(g, k):
        return remote(
            near_out.at[k, :, half(g)], near_in.at[k, :, half(g)],
            near_send.at[g, k], near_recv.at[g, k], along(near[k]),
        )

    def piece_of(d):
        return (a + d + 4 + r + 2 * c) % 4

    def rows_in(i, size=PIECE):
        return pl.ds(pl.multiple_of(i * PIECE, PIECE), size)

    def sized(i, act):
        @pl.when(i == 3)
        def _():
            act(PIECE // 2)

        @pl.when(i != 3)
        def _():
            act(PIECE)

    def far_copy(g, k, size):
        return remote(
            far_out.at[rows_in(piece_of(k + 1), size), half(g)],
            far_in.at[k, pl.ds(0, size), half(g)],
            far_send.at[g, k], far_recv.at[g, k], along(4 * (k + 1)),
        )

    def mine():
        return rows_in(piece_of(0))

    def gf_copy(g, k, size):
        piece = gram.at[c, r, rows_in(piece_of(0), size), half(g)]
        return remote(piece, piece, gf_send.at[g, k], gf_recv.at[g, k], along(4 * (k + 1)))

    def gf_arrived(g, k, size):
        arrived(gram.at[c, r, rows_in(piece_of(-1 - k), size), half(g)], gf_recv.at[g, k])

    def quarter_of(core, q, g):
        return gram.at[core, q, pl.ds(0, PART), half(g)]

    def gn_copy(g, k):
        part = quarter_of(c, r, g)
        return remote(part, part, gn_send.at[g, k], gn_recv.at[g, k], along(near[k]))

    def hand(g, k):
        part = quarter_of(c, (r + k) % 4, g)
        return remote(part, part, h_send.at[g, k], h_recv.at[g, k], sibling)

    cls[PART:] = jnp.zeros_like(cls[PART:])
    for g in range(2):
        s_copy(g).wait_recv()
        for k in (2, 0, 1):
            q = (r + near[k] + 4) % 4
            near_out[k, :, half(g)] = (
                acc[q, :, half(g)] + sib_in[q, :, half(g)].astype(f32)
            ).astype(bf16)
            near_copy(g, k).start()
        cls[0:PART, half(g)] = acc[r, :, half(g)] + sib_in[r, :, half(g)].astype(f32)
    pl.semaphore_wait(inside.at[1], 2)
    for g in range(2):
        for k in (0, 1, 2):
            near_copy(g, k).wait_recv()
        cls[0:PART, half(g)] += (
            near_in[0, :, half(g)].astype(f32)
            + near_in[1, :, half(g)].astype(f32)
            + near_in[2, :, half(g)].astype(f32)
        )
        far_out[:, half(g)] = cls[:, half(g)].astype(bf16)
        for k in (1, 0, 2):
            sized(piece_of(k + 1), lambda n: far_copy(g, k, n).start())

    for g in range(2):
        total = cls[mine(), half(g)]
        for k in (0, 2, 1):
            sized(piece_of(0), lambda n: far_copy(g, k, n).wait_recv())
            total += far_in[k, :, half(g)].astype(f32)
        gram[c, r, mine(), half(g)] = total.astype(bf16)
        for k in (1, 0, 2):
            sized(piece_of(0), lambda n: gf_copy(g, k, n).start())
    for g in range(2):
        for k in (0, 2, 1):
            sized(piece_of(-1 - k), lambda n: gf_arrived(g, k, n))
        for k in (2, 0, 1):
            gn_copy(g, k).start()
        hand(g, 0).start()

    def share(g):
        return pl.ds(*SHARES[g])

    def rows_of(g, q):
        first, size = HALVES[g][0], SHARES[g][1]
        return pl.ds(pl.multiple_of(first + q * size, PIECE), size)

    def rows_at(q):
        return pl.ds(pl.multiple_of(q * ROWS, ROWS), ROWS)

    def gram_rows(q):
        return gram[q // 2, pl.ds((q % 2) * 2, 2), 0:PART].reshape(ROWS, BLOCK)

    def dot(left, right):
        return jnp.dot(left, right, preferred_element_type=f32)

    def tx_copy(g, n, k):
        return remote(
            tx_out.at[k, share(g), SPLIT[n]], tx_in.at[k, share(g), SPLIT[n]],
            tx_send.at[g, n, k], tx_recv.at[g, n, k], on_x(k),
        )

    def second(n):
        return pl.ds(SECOND.start + SPLIT[n].start, SPLIT[n].size)

    def strip(f):
        return pl.ds(f * STRIP, STRIP)

    def ty_copy(f, k):
        return remote(
            ty_out.at[k, :, strip(f)], ty_in.at[k, :, strip(f)],
            ty_send.at[f, k], ty_recv.at[f, k], on_y(k),
        )

    for g in range(2):
        for k in (0, 1, 2):
            arrived(quarter_of(c, (r - near[k] + 4) % 4, g), gn_recv.at[g, k])
            hand(g, (3, 1, 2)[k]).start()
        for k in (0, 3, 1, 2):
            arrived(quarter_of(1 - c, (r + k) % 4, g), h_recv.at[g, k])
        if g == 1:
            for f in range(2):
                for k in (2, 1, 3):
                    ty_out[k, :, strip(f)] = dot(
                        gram_rows((y + k) % SIDE), xj[:, strip(f)]
                    ).astype(bf16)
                    ty_copy(f, k).start()
        gram_t[half(g)] = gram[:, :, 0:PART, half(g)].reshape(BLOCK, HALVES[g][1]).T
        for n in range(2):
            for k in (2, 1, 3):
                tx_out[k, share(g), SPLIT[n]] = dot(
                    gram_t[rows_of(g, (x + k) % SIDE)], xi[:, second(n)]
                ).astype(bf16)
                tx_copy(g, n, k).start()
        tx_sum[share(g)] = dot(gram_t[rows_of(g, x)], xi[:, SECOND])

    def ux_copy(g, n, k):
        here = ux.at[rows_of(g, x), SPLIT[n]]
        return remote(here, here, ux_send.at[g, n, k], ux_recv.at[g, n, k], on_x(k))

    def uy_copy(f, k):
        here = uy.at[rows_at(y), strip(f)]
        return remote(here, here, uy_send.at[f, k], uy_recv.at[f, k], on_y(k))

    def ux_part(g, n):
        total = tx_sum[share(g), SPLIT[n]]
        for k in (1, 3, 2):
            tx_copy(g, n, k).wait_recv()
            total += tx_in[k, share(g), SPLIT[n]].astype(f32)
        ux[rows_of(g, x), SPLIT[n]] = (
            coef_quad * xj[rows_of(g, x), second(n)].astype(f32) + coef_cubic * total
        ).astype(bf16)
        for k in (2, 1, 3):
            ux_copy(g, n, k).start()

    ux_part(0, 0)
    ux_part(0, 1)
    for f in range(2):
        total = dot(gram_rows(y), xj[:, strip(f)])
        for k in (1, 3, 2):
            ty_copy(f, k).wait_recv()
            total += ty_in[k, :, strip(f)].astype(f32)
        uy[rows_at(y), strip(f)] = (
            coef_quad * xi[rows_at(y), strip(f)].astype(f32) + coef_cubic * total
        ).astype(bf16)
        for k in (2, 1, 3):
            uy_copy(f, k).start()
        ux_part(1, f)

    def px_copy(f, k):
        return remote(
            px_out.at[k, :, strip(f)], px_in.at[k, :, strip(f)],
            px_send.at[f, k], px_recv.at[f, k], on_x(k),
        )

    def py_copy(n, q):
        return remote(
            py_out.at[q, :, SPLIT[n]], py_in.at[y, :, SPLIT[n]],
            py_send.at[n, q], py_recv.at[n, y], from_i(q),
        )

    for f in range(2):
        for k in (1, 3, 2):
            arrived(uy.at[rows_at((y + SIDE - k) % SIDE), strip(f)], uy_recv.at[f, k])
        for k in (2, 1, 3):
            px_out[k, :, strip(f)] = dot(
                gram_t[rows_at((x + k) % SIDE)], uy[:, strip(f)]
            ).astype(bf16)
            px_copy(f, k).start()
        for g in range(2):
            for k in (1, 3, 2):
                arrived(ux.at[rows_of(g, (x + SIDE - k) % SIDE), SPLIT[f]], ux_recv.at[g, f, k])
        for q in range(SIDE):
            local = jnp.logical_and(own, q == quarter)
            py_out[q, :, SPLIT[f]] = dot(gram_rows(q), ux[:, SPLIT[f]]).astype(bf16)

            @pl.when(local)
            def _():
                pltpu.make_async_copy(
                    py_out.at[q, :, SPLIT[f]], py_in.at[y, :, SPLIT[f]], py_recv.at[f, y]
                ).start()

            @pl.when(jnp.logical_not(local))
            def _():
                py_copy(f, q).start()

    factor = math.sqrt(max(M, N))

    def fin_copy(f):
        part = strip(f)
        return remote(
            fin_out.at[:, part], fin_in.at[:, part], fin_send.at[f], fin_recv.at[f], peer
        )

    for f in range(2):
        total = dot(gram_t[rows_at(x)], uy[:, strip(f)])
        total += coef_linear * xj[rows_at(x), strip(f)].astype(f32)
        for k in (1, 3, 2):
            px_copy(f, k).wait_recv()
            total += px_in[k, :, strip(f)].astype(f32)
        fin_out[:, strip(f)] = (total * factor).astype(bf16)

        @pl.when(others)
        def _():
            fin_copy(f).start()

    @pl.when(own)
    def _():
        out_ref[:, FIRST] = fin_out[...]

    swap_copy.wait_send()
    hand_i(m_ref).wait_send()
    for k in (1, 3):
        i_copy(k).wait_send()
    for k in (1, 2, 3):
        j_copy(m_ref, k).wait_send()
    for g in range(2):
        s_copy(g).wait_send()
        for k in range(3):
            near_copy(g, k).wait_send()
            sized(piece_of(k + 1), lambda n: far_copy(g, k, n).wait_send())
            sized(piece_of(0), lambda n: gf_copy(g, k, n).wait_send())
            gn_copy(g, k).wait_send()
        for k in range(4):
            hand(g, k).wait_send()
        for k in (1, 2, 3):
            for n in range(2):
                tx_copy(g, n, k).wait_send()
                ux_copy(g, n, k).wait_send()
    for f in range(2):
        for k in (1, 2, 3):
            ty_copy(f, k).wait_send()
            uy_copy(f, k).wait_send()
            px_copy(f, k).wait_send()

    for n in range(2):
        result = coef_linear * m_ref[:, second(n)].astype(f32)
        for k in range(SIDE):
            arrived(py_in.at[k, :, SPLIT[n]], py_recv.at[n, k])
            result += py_in[k, :, SPLIT[n]].astype(f32)
        out_ref[:, second(n)] = (result * factor).astype(bf16)

    @pl.when(others)
    def _():
        for f in range(2):
            fin_copy(f).wait_recv()
            out_ref[:, strip(f)] = fin_in[:, strip(f)]
            fin_copy(f).wait_send()

    for n in range(2):
        for q in range(SIDE):

            @pl.when(jnp.logical_not(jnp.logical_and(own, q == quarter)))
            def _():
                py_copy(n, q).wait_send()


def body(momentum):
    bf16, f32 = jnp.bfloat16, jnp.float32
    first = (SIDE, ROWS, FIRST.size)
    second = (SIDE, ROWS, SECOND.size)
    sem = pltpu.SemaphoreType.DMA
    return pl.pallas_call(
        kernel,
        out_shape=jax.ShapeDtypeStruct((ROWS, COLS), bf16),
        in_specs=[pl.BlockSpec(memory_space=pltpu.VMEM)],
        out_specs=pl.BlockSpec(memory_space=pltpu.VMEM),
        scratch_shapes=[
            pltpu.VMEM((ROWS, COLS), bf16),
            pltpu.VMEM((BLOCK, COLS), bf16),
            pltpu.VMEM((BLOCK, COLS), bf16),
            pltpu.VMEM((4, PART, BLOCK), f32),
            pltpu.VMEM((4, PART, BLOCK), bf16),
            pltpu.VMEM((4, PART, BLOCK), bf16),
            pltpu.VMEM((3, PART, BLOCK), bf16),
            pltpu.VMEM((3, PART, BLOCK), bf16),
            pltpu.VMEM((PADDED, BLOCK), f32),
            pltpu.VMEM((PADDED, BLOCK), bf16),
            pltpu.VMEM((3, PIECE, BLOCK), bf16),
            pltpu.VMEM((2, 4, PADDED, BLOCK), bf16),
            pltpu.VMEM((BLOCK, BLOCK), bf16),
            pltpu.VMEM(second, bf16),
            pltpu.VMEM(second, bf16),
            pltpu.VMEM(second[1:], f32),
            pltpu.VMEM(first, bf16),
            pltpu.VMEM(first, bf16),
            pltpu.VMEM((BLOCK, SECOND.size), bf16),
            pltpu.VMEM((BLOCK, FIRST.size), bf16),
            pltpu.VMEM(first, bf16),
            pltpu.VMEM(first, bf16),
            pltpu.VMEM(second, bf16),
            pltpu.VMEM(second, bf16),
            pltpu.VMEM(first[1:], bf16),
            pltpu.VMEM(first[1:], bf16),
            sem((SIDE,)), sem((SIDE,)),
            sem((SIDE,)), sem((SIDE,)),
            sem((2,)), sem((2,)),
            sem((2, 3)), sem((2, 3)),
            sem((2, 3)), sem((2, 3)),
            sem((2, 3)), sem((2, 3)),
            sem((2, 3)), sem((2, 3)),
            sem((2, 4)), sem((2, 4)),
            sem((1,)), sem((1,)),
            sem((2, 2, SIDE)), sem((2, 2, SIDE)),
            sem((2, SIDE)), sem((2, SIDE)),
            sem((2, 2, SIDE)), sem((2, 2, SIDE)),
            sem((2, SIDE)), sem((2, SIDE)),
            sem((2, SIDE)), sem((2, SIDE)),
            sem((2, SIDE)), sem((2, SIDE)),
            sem((2,)), sem((2,)),
            pltpu.SemaphoreType.REGULAR((2,)),
        ],
        compiler_params=pltpu.CompilerParams(
            collective_id=0, has_side_effects=True, vmem_limit_bytes=48 * 2**20
        ),
        cost_estimate=pl.CostEstimate(
            flops=6 * BLOCK * BLOCK * COLS, bytes_accessed=4 * ROWS * COLS, transcendentals=0
        ),
        name="newton_schulz",
    )(momentum)


def solution(mesh):
    return jax.shard_map(
        body,
        mesh=mesh,
        in_specs=(P("row", "col"),),
        out_specs=P("row", "col"),
        check_vma=False,
    )
```

```python
import math

import jax
import jax.numpy as jnp
from jax import lax
from jax.experimental import pallas as pl
from jax.experimental.pallas import tpu as pltpu
from jax.sharding import PartitionSpec as P

M = 3584
N = 18432

coef_linear = 3.4445
coef_quad = -4.775
coef_cubic = 2.0315

SIDE = 4
DEPTH = 16
BLOCK = M // SIDE
ROWS = BLOCK // SIDE
COLS = N // 32
PART = ROWS // 2
PIECE = 32
PADDED = 4 * PIECE
HALVES = ((0, 512), (512, BLOCK - 512))
SHARES = ((0, 128), (128, ROWS - 128))
FIRST = pl.ds(0, 256)
STRIP = 128
SECOND = pl.ds(256, COLS - 256)
SPLIT = (pl.ds(0, 128), pl.ds(128, COLS - 384))
NT = (((1,), (1,)), ((), ()))


def kernel(
    m_ref, out_ref, swap, xi, xj, acc, sib_out, sib_in, near_out, near_in, cls, far_out, far_in,
    gram, gram_t, tx_out, tx_in, tx_sum, ty_out, ty_in, ux, uy, px_out, px_in, py_out, py_in,
    fin_out, fin_in,
    i_send, i_recv, j_send, j_recv, s_send, s_recv, near_send, near_recv, far_send, far_recv,
    gf_send, gf_recv, gn_send, gn_recv, h_send, h_recv, w_send, w_recv,
    tx_send, tx_recv, ty_send, ty_recv, ux_send, ux_recv, uy_send, uy_recv,
    px_send, px_recv, py_send, py_recv, fin_send, fin_recv, inside,
):
    row, col = lax.axis_index("row"), lax.axis_index("col")
    x, y_lo, c = row // 4, (row // 2) % 2, row % 2
    z, y_hi = col // 2, col % 2
    y = y_hi * 2 + y_lo
    quarter = y_lo * 2 + c
    r, a = z % 4, z // 4
    bf16, f32 = jnp.bfloat16, jnp.float32

    def at(x_, y_, c_):
        return ((x_ * 2 + y_ % 2) * 2 + c_, z * 2 + y_ // 2)

    def along(d):
        return (row, ((z + d + DEPTH) % DEPTH) * 2 + y_hi)

    def remote(src, dst, send, recv, where):
        return pltpu.make_async_remote_copy(
            src_ref=src, dst_ref=dst, send_sem=send, recv_sem=recv,
            device_id=where, device_id_type=pl.DeviceIdType.MESH,
        )

    def arrived(dst, recv):
        pltpu.make_async_copy(dst, dst, recv).wait()

    def to_i(k):
        return at(x, k, y_hi)

    def from_i(k):
        return at(x, c * 2 + k // 2, k % 2)

    def on_x(k):
        return at((x + k) % SIDE, y, c)

    def on_y(k):
        return at(x, (y + k) % SIDE, c)

    sibling = at(x, y, 1 - c)
    peer = at(x, (y + 2) % SIDE, 1 - c)
    own = c == y_hi
    others = jnp.logical_not(own)
    near = (1, -1, 2 - 4 * c)

    barrier = pltpu.get_barrier_semaphore()

    def signal(where):
        pl.semaphore_signal(barrier, inc=1, device_id=where, device_id_type=pl.DeviceIdType.MESH)

    for d in (2, -2, 1, -1):
        signal(along(d))
    for k in (2, 1, 3):
        signal(on_x(k))
        signal(on_y(k))
    for k in range(SIDE):

        @pl.when(jnp.logical_not(jnp.logical_and(own, y == k)))
        def _():
            signal(to_i(k))

        @pl.when(jnp.logical_not(jnp.logical_and(own, quarter == k)))
        def _():
            signal(from_i(k))

    signal(peer)
    signal(sibling)
    pl.semaphore_wait(barrier, 20 - 2 * own.astype(jnp.int32))

    def pass_on(k, d):
        for e in (d, -d):
            pl.semaphore_signal(
                inside.at[k], inc=1, device_id=along(e), device_id_type=pl.DeviceIdType.MESH
            )

    pass_on(0, 2)

    def block(ref, k):
        return ref.at[pl.ds(pl.multiple_of(k * ROWS, ROWS), ROWS)]

    common = y_lo * 2 + y_hi
    handed = y_lo * 2 + 1 - y_hi
    swap_copy = remote(m_ref, swap, w_send.at[0], w_recv.at[0], peer)

    def hand_i(src):
        return remote(src, block(xi, handed), i_send.at[0], i_recv.at[handed], sibling)

    def i_copy(k):
        there = block(xi, quarter)
        return remote(m_ref, there, i_send.at[k], i_recv.at[quarter], to_i((y + k) % SIDE))

    def j_copy(src, k):
        return remote(src, block(xj, x), j_send.at[k], j_recv.at[k], on_x(k))

    def keep(src):
        common_rows = pl.ds(pl.multiple_of(common * ROWS, ROWS), ROWS)
        xi[common_rows] = src[...]
        x_rows = pl.ds(pl.multiple_of(x * ROWS, ROWS), ROWS)
        xj[x_rows] = src[...]

    swap_copy.start()

    @pl.when(own)
    def _():
        for k in (2, 1, 3):
            j_copy(m_ref, k).start()
        for k in (1, 3):
            i_copy(k).start()
        keep(m_ref)

    @pl.when(others)
    def _():
        hand_i(m_ref).start()

    swap_copy.wait_recv()

    @pl.when(own)
    def _():
        hand_i(swap).start()

    @pl.when(others)
    def _():
        for k in (2, 1, 3):
            j_copy(swap, k).start()
        for k in (1, 3):
            i_copy(k).start()

    @pl.when(others)
    def _():
        keep(swap)

    arrived(block(xi, handed), i_recv.at[handed])
    for k in range(2):
        far_slot = (1 - y_lo) * 2 + k
        arrived(block(xi, far_slot), i_recv.at[far_slot])
    for k in (1, 2, 3):
        arrived(block(xj, (x + SIDE - k) % SIDE), j_recv.at[k])

    pl.semaphore_wait(inside.at[0], 2)
    pass_on(1, 4)

    def half(g):
        return pl.ds(*HALVES[g])

    def s_copy(g):
        return remote(
            sib_out.at[:, :, half(g)], sib_in.at[:, :, half(g)], s_send.at[g], s_recv.at[g], sibling
        )

    def terms(core, g):
        rows = pl.ds(pl.multiple_of(core * (BLOCK // 2), BLOCK // 2), BLOCK // 2)
        return lax.dot_general(xi[rows], xj[half(g)], NT, preferred_element_type=f32).reshape(
            4, PART, HALVES[g][1]
        )

    for g in range(2):
        sib_out[:, :, half(g)] = terms(1 - c, g).astype(bf16)
        s_copy(g).start()
        acc[:, :, half(g)] = terms(c, g)

    def near_copy(g, k):
        return remote(
            near_out.at[k, :, half(g)], near_in.at[k, :, half(g)],
            near_send.at[g, k], near_recv.at[g, k], along(near[k]),
        )

    def piece_of(d):
        return (a + d + 4 + r + 2 * c) % 4

    def rows_in(i, size=PIECE):
        return pl.ds(pl.multiple_of(i * PIECE, PIECE), size)

    def sized(i, act):
        @pl.when(i == 3)
        def _():
            act(PIECE // 2)

        @pl.when(i != 3)
        def _():
            act(PIECE)

    def far_copy(g, k, size):
        return remote(
            far_out.at[rows_in(piece_of(k + 1), size), half(g)],
            far_in.at[k, pl.ds(0, size), half(g)],
            far_send.at[g, k], far_recv.at[g, k], along(4 * (k + 1)),
        )

    def mine():
        return rows_in(piece_of(0))

    def gf_copy(g, k, size):
        piece = gram.at[c, r, rows_in(piece_of(0), size), half(g)]
        return remote(piece, piece, gf_send.at[g, k], gf_recv.at[g, k], along(4 * (k + 1)))

    def gf_arrived(g, k, size):
        arrived(gram.at[c, r, rows_in(piece_of(-1 - k), size), half(g)], gf_recv.at[g, k])

    def quarter_of(core, q, g):
        return gram.at[core, q, pl.ds(0, PART), half(g)]

    def gn_copy(g, k):
        part = quarter_of(c, r, g)
        return remote(part, part, gn_send.at[g, k], gn_recv.at[g, k], along(near[k]))

    def hand(g, k):
        part = quarter_of(c, (r + k) % 4, g)
        return remote(part, part, h_send.at[g, k], h_recv.at[g, k], sibling)

    cls[PART:] = jnp.zeros_like(cls[PART:])
    for g in range(2):
        s_copy(g).wait_recv()
        for k in (2, 0, 1):
            q = (r + near[k] + 4) % 4
            near_out[k, :, half(g)] = (
                acc[q, :, half(g)] + sib_in[q, :, half(g)].astype(f32)
            ).astype(bf16)
            near_copy(g, k).start()
        cls[0:PART, half(g)] = acc[r, :, half(g)] + sib_in[r, :, half(g)].astype(f32)
    pl.semaphore_wait(inside.at[1], 2)
    for g in range(2):
        for k in (0, 1, 2):
            near_copy(g, k).wait_recv()
        cls[0:PART, half(g)] += (
            near_in[0, :, half(g)].astype(f32)
            + near_in[1, :, half(g)].astype(f32)
            + near_in[2, :, half(g)].astype(f32)
        )
        far_out[:, half(g)] = cls[:, half(g)].astype(bf16)
        for k in (1, 0, 2):
            sized(piece_of(k + 1), lambda n: far_copy(g, k, n).start())

    for g in range(2):
        total = cls[mine(), half(g)]
        for k in (0, 2, 1):
            sized(piece_of(0), lambda n: far_copy(g, k, n).wait_recv())
            total += far_in[k, :, half(g)].astype(f32)
        gram[c, r, mine(), half(g)] = total.astype(bf16)
        for k in (1, 0, 2):
            sized(piece_of(0), lambda n: gf_copy(g, k, n).start())
    for g in range(2):
        for k in (0, 2, 1):
            sized(piece_of(-1 - k), lambda n: gf_arrived(g, k, n))
        for k in (2, 0, 1):
            gn_copy(g, k).start()
        hand(g, 0).start()

    def share(g):
        return pl.ds(*SHARES[g])

    def rows_of(g, q):
        first, size = HALVES[g][0], SHARES[g][1]
        return pl.ds(pl.multiple_of(first + q * size, PIECE), size)

    def rows_at(q):
        return pl.ds(pl.multiple_of(q * ROWS, ROWS), ROWS)

    def gram_rows(q):
        return gram[q // 2, pl.ds((q % 2) * 2, 2), 0:PART].reshape(ROWS, BLOCK)

    def dot(left, right):
        return jnp.dot(left, right, preferred_element_type=f32)

    def tx_copy(g, n, k):
        return remote(
            tx_out.at[k, share(g), SPLIT[n]], tx_in.at[k, share(g), SPLIT[n]],
            tx_send.at[g, n, k], tx_recv.at[g, n, k], on_x(k),
        )

    def second(n):
        return pl.ds(SECOND.start + SPLIT[n].start, SPLIT[n].size)

    def strip(f):
        return pl.ds(f * STRIP, STRIP)

    def ty_copy(f, k):
        return remote(
            ty_out.at[k, :, strip(f)], ty_in.at[k, :, strip(f)],
            ty_send.at[f, k], ty_recv.at[f, k], on_y(k),
        )

    for g in range(2):
        for k in (0, 1, 2):
            arrived(quarter_of(c, (r - near[k] + 4) % 4, g), gn_recv.at[g, k])
            hand(g, (3, 1, 2)[k]).start()
        for k in (0, 3, 1, 2):
            arrived(quarter_of(1 - c, (r + k) % 4, g), h_recv.at[g, k])
        if g == 1:
            for f in range(2):
                for k in (2, 1, 3):
                    ty_out[k, :, strip(f)] = dot(
                        gram_rows((y + k) % SIDE), xj[:, strip(f)]
                    ).astype(bf16)
                    ty_copy(f, k).start()
        gram_t[half(g)] = gram[:, :, 0:PART, half(g)].reshape(BLOCK, HALVES[g][1]).T
        for n in range(2):
            for k in (2, 1, 3):
                tx_out[k, share(g), SPLIT[n]] = dot(
                    gram_t[rows_of(g, (x + k) % SIDE)], xi[:, second(n)]
                ).astype(bf16)
                tx_copy(g, n, k).start()
        tx_sum[share(g)] = dot(gram_t[rows_of(g, x)], xi[:, SECOND])

    def ux_copy(g, n, k):
        here = ux.at[rows_of(g, x), SPLIT[n]]
        return remote(here, here, ux_send.at[g, n, k], ux_recv.at[g, n, k], on_x(k))

    def uy_copy(f, k):
        here = uy.at[rows_at(y), strip(f)]
        return remote(here, here, uy_send.at[f, k], uy_recv.at[f, k], on_y(k))

    def ux_part(g, n):
        total = tx_sum[share(g), SPLIT[n]]
        for k in (1, 3, 2):
            tx_copy(g, n, k).wait_recv()
            total += tx_in[k, share(g), SPLIT[n]].astype(f32)
        ux[rows_of(g, x), SPLIT[n]] = (
            coef_quad * xj[rows_of(g, x), second(n)].astype(f32) + coef_cubic * total
        ).astype(bf16)
        for k in (2, 1, 3):
            ux_copy(g, n, k).start()

    ux_part(0, 0)
    ux_part(0, 1)
    for f in range(2):
        total = dot(gram_rows(y), xj[:, strip(f)])
        for k in (1, 3, 2):
            ty_copy(f, k).wait_recv()
            total += ty_in[k, :, strip(f)].astype(f32)
        uy[rows_at(y), strip(f)] = (
            coef_quad * xi[rows_at(y), strip(f)].astype(f32) + coef_cubic * total
        ).astype(bf16)
        for k in (2, 1, 3):
            uy_copy(f, k).start()
        ux_part(1, f)

    def px_copy(f, k):
        return remote(
            px_out.at[k, :, strip(f)], px_in.at[k, :, strip(f)],
            px_send.at[f, k], px_recv.at[f, k], on_x(k),
        )

    def py_copy(n, q):
        return remote(
            py_out.at[q, :, SPLIT[n]], py_in.at[y, :, SPLIT[n]],
            py_send.at[n, q], py_recv.at[n, y], from_i(q),
        )

    for f in range(2):
        for k in (1, 3, 2):
            arrived(uy.at[rows_at((y + SIDE - k) % SIDE), strip(f)], uy_recv.at[f, k])
        for k in (2, 1, 3):
            px_out[k, :, strip(f)] = dot(
                gram_t[rows_at((x + k) % SIDE)], uy[:, strip(f)]
            ).astype(bf16)
            px_copy(f, k).start()
        for g in range(2):
            for k in (1, 3, 2):
                arrived(ux.at[rows_of(g, (x + SIDE - k) % SIDE), SPLIT[f]], ux_recv.at[g, f, k])
        for q in range(SIDE):
            local = jnp.logical_and(own, q == quarter)
            py_out[q, :, SPLIT[f]] = dot(gram_rows(q), ux[:, SPLIT[f]]).astype(bf16)

            @pl.when(local)
            def _():
                pltpu.make_async_copy(
                    py_out.at[q, :, SPLIT[f]], py_in.at[y, :, SPLIT[f]], py_recv.at[f, y]
                ).start()

            @pl.when(jnp.logical_not(local))
            def _():
                py_copy(f, q).start()

    factor = math.sqrt(max(M, N))

    def fin_copy(f):
        part = strip(f)
        return remote(
            fin_out.at[:, part], fin_in.at[:, part], fin_send.at[f], fin_recv.at[f], peer
        )

    for f in range(2):
        total = dot(gram_t[rows_at(x)], uy[:, strip(f)])
        total += coef_linear * xj[rows_at(x), strip(f)].astype(f32)
        for k in (1, 3, 2):
            px_copy(f, k).wait_recv()
            total += px_in[k, :, strip(f)].astype(f32)
        fin_out[:, strip(f)] = (total * factor).astype(bf16)

        @pl.when(others)
        def _():
            fin_copy(f).start()

    @pl.when(own)
    def _():
        out_ref[:, FIRST] = fin_out[...]

    swap_copy.wait_send()
    hand_i(m_ref).wait_send()
    for k in (1, 3):
        i_copy(k).wait_send()
    for k in (1, 2, 3):
        j_copy(m_ref, k).wait_send()
    for g in range(2):
        s_copy(g).wait_send()
        for k in range(3):
            near_copy(g, k).wait_send()
            sized(piece_of(k + 1), lambda n: far_copy(g, k, n).wait_send())
            sized(piece_of(0), lambda n: gf_copy(g, k, n).wait_send())
            gn_copy(g, k).wait_send()
        for k in range(4):
            hand(g, k).wait_send()
        for k in (1, 2, 3):
            for n in range(2):
                tx_copy(g, n, k).wait_send()
                ux_copy(g, n, k).wait_send()
    for f in range(2):
        for k in (1, 2, 3):
            ty_copy(f, k).wait_send()
            uy_copy(f, k).wait_send()
            px_copy(f, k).wait_send()

    for n in range(2):
        result = coef_linear * m_ref[:, second(n)].astype(f32)
        for k in range(SIDE):
            arrived(py_in.at[k, :, SPLIT[n]], py_recv.at[n, k])
            result += py_in[k, :, SPLIT[n]].astype(f32)
        out_ref[:, second(n)] = (result * factor).astype(bf16)

    @pl.when(others)
    def _():
        for f in range(2):
            fin_copy(f).wait_recv()
            out_ref[:, strip(f)] = fin_in[:, strip(f)]
            fin_copy(f).wait_send()

    for n in range(2):
        for q in range(SIDE):

            @pl.when(jnp.logical_not(jnp.logical_and(own, q == quarter)))
            def _():
                py_copy(n, q).wait_send()


def body(momentum):
    bf16, f32 = jnp.bfloat16, jnp.float32
    first = (SIDE, ROWS, FIRST.size)
    second = (SIDE, ROWS, SECOND.size)
    sem = pltpu.SemaphoreType.DMA
    return pl.pallas_call(
        kernel,
        out_shape=jax.ShapeDtypeStruct((ROWS, COLS), bf16),
        in_specs=[pl.BlockSpec(memory_space=pltpu.VMEM)],
        out_specs=pl.BlockSpec(memory_space=pltpu.VMEM),
        scratch_shapes=[
            pltpu.VMEM((ROWS, COLS), bf16),
            pltpu.VMEM((BLOCK, COLS), bf16),
            pltpu.VMEM((BLOCK, COLS), bf16),
            pltpu.VMEM((4, PART, BLOCK), f32),
            pltpu.VMEM((4, PART, BLOCK), bf16),
            pltpu.VMEM((4, PART, BLOCK), bf16),
            pltpu.VMEM((3, PART, BLOCK), bf16),
            pltpu.VMEM((3, PART, BLOCK), bf16),
            pltpu.VMEM((PADDED, BLOCK), f32),
            pltpu.VMEM((PADDED, BLOCK), bf16),
            pltpu.VMEM((3, PIECE, BLOCK), bf16),
            pltpu.VMEM((2, 4, PADDED, BLOCK), bf16),
            pltpu.VMEM((BLOCK, BLOCK), bf16),
            pltpu.VMEM(second, bf16),
            pltpu.VMEM(second, bf16),
            pltpu.VMEM(second[1:], f32),
            pltpu.VMEM(first, bf16),
            pltpu.VMEM(first, bf16),
            pltpu.VMEM((BLOCK, SECOND.size), bf16),
            pltpu.VMEM((BLOCK, FIRST.size), bf16),
            pltpu.VMEM(first, bf16),
            pltpu.VMEM(first, bf16),
            pltpu.VMEM(second, bf16),
            pltpu.VMEM(second, bf16),
            pltpu.VMEM(first[1:], bf16),
            pltpu.VMEM(first[1:], bf16),
            sem((SIDE,)), sem((SIDE,)),
            sem((SIDE,)), sem((SIDE,)),
            sem((2,)), sem((2,)),
            sem((2, 3)), sem((2, 3)),
            sem((2, 3)), sem((2, 3)),
            sem((2, 3)), sem((2, 3)),
            sem((2, 3)), sem((2, 3)),
            sem((2, 4)), sem((2, 4)),
            sem((1,)), sem((1,)),
            sem((2, 2, SIDE)), sem((2, 2, SIDE)),
            sem((2, SIDE)), sem((2, SIDE)),
            sem((2, 2, SIDE)), sem((2, 2, SIDE)),
            sem((2, SIDE)), sem((2, SIDE)),
            sem((2, SIDE)), sem((2, SIDE)),
            sem((2, SIDE)), sem((2, SIDE)),
            sem((2,)), sem((2,)),
            pltpu.SemaphoreType.REGULAR((2,)),
        ],
        compiler_params=pltpu.CompilerParams(
            collective_id=0, has_side_effects=True, vmem_limit_bytes=48 * 2**20
        ),
        cost_estimate=pl.CostEstimate(
            flops=6 * BLOCK * BLOCK * COLS, bytes_accessed=4 * ROWS * COLS, transcendentals=0
        ),
        name="newton_schulz",
    )(momentum)


def solution(mesh):
    return jax.shard_map(
        body,
        mesh=mesh,
        in_specs=(P("row", "col"),),
        out_specs=P("row", "col"),
        check_vma=False,
    )
```
